256 devices in a mesh: sp: 16 (over x, y), blk: 16 (over z, core).
Axes of the slice: x: 4, y: 4, z: 8, core: 2. Of those that a mesh axis runs over, the one named last changes fastest.
Arguments:
- queries: bfloat16 [32768, 8192], P(('blk', 'sp')), may hold values from -120 to 120
- key_state_rows: bfloat16 [32768, 1024], P(('blk', 'sp')), may hold values from -6 to 6
- value_state_rows: bfloat16 [32768, 1024], P(('blk', 'sp')), may hold values from -6 to 6
- cotangent: bfloat16 [32768, 8192], P(('blk', 'sp')), may hold values from -6 to 6
- block_list: int32 [256, 1], replicated, may hold values from 0 to 255, as said below
- query_exponent: int32 [256, 64], P('blk'), may hold values from -5 to 1
- key_block_exponent: int32 [256, 8], P('blk'), may hold values from -5 to 1
- value_block_exponent: int32 [256, 8], P('blk'), may hold values from -5 to 1
Outputs:
- attention: bfloat16 [32768, 8192], P(('blk', 'sp'))
- query_gradient_rows: bfloat16 [32768, 8192], P(('blk', 'sp'))
- key_gradient_rows: bfloat16 [32768, 1024], P(('blk', 'sp'))
- value_gradient_rows: bfloat16 [32768, 1024], P(('blk', 'sp'))
The draws below stay inside these ranges and needn't reach their ends.
Inputs may be any that keep to these rules, and one draw needn't show every extreme that they name: Each entry of block_list is the block of its own row or an earlier block. `block_list`: group the query blocks 16 at a time in order (the blocks held along one index of blk). Among the 16 entries of one group, at most 2 name blocks of any one other group and differ from their own row's block; in every draw some pair of groups reaches 2.
All inputs are finite; a program needn't handle non-finite values.
Results may differ from the reference program's by a relative error of at most 0.012.
Values may be sent and summed in bfloat16 or wider, within the bound.
No kernel may reach another device: no remote copies, remote signals or barrier semaphores. Data moves between devices by JAX's collectives and lax.ppermute only.
A program may use at most 128 MiB of HBM per device.

```python
import math
import jax
import jax.numpy as jnp
from jax import lax

QUERY_HEAD_COUNT = 64
KEY_VALUE_HEADS = 8
HEAD_SIZE = 128
BLOCK = 128
LIST = 1
CAP = 2
QB_DEV = 16
TOKEN_BLOCKS = 256
SEQUENCE_LENGTH = 32768
N_SP = 16
N_BLK = 16


def shared_keys(key):
    return jax.random.normal(jax.random.fold_in(key, 7), (SEQUENCE_LENGTH, KEY_VALUE_HEADS, HEAD_SIZE), jnp.float32)


def draw_key_state_rows(key, part):
    base_key_rows = shared_keys(key)
    return jnp.clip(base_key_rows, -6.0, 6.0).reshape(SEQUENCE_LENGTH, KEY_VALUE_HEADS * HEAD_SIZE).astype(jnp.bfloat16)


def draw_queries(key, part):
    key = jax.random.fold_in(key, 5)
    drawn = jax.random.normal(key, (SEQUENCE_LENGTH, QUERY_HEAD_COUNT, HEAD_SIZE), jnp.float32)
    return jnp.clip(drawn, -6.0, 6.0).reshape(SEQUENCE_LENGTH, QUERY_HEAD_COUNT * HEAD_SIZE).astype(jnp.bfloat16)


def permute_row(row_key):
    return jax.random.permutation(row_key, QB_DEV * LIST)


def draw_block_list(key, part):
    key = jax.random.fold_in(key, 9)
    entries = QB_DEV * LIST
    key_perm, key_offset, key_remote, key_local = jax.random.split(key, 4)
    slot_order = jax.vmap(permute_row)(jax.random.split(key_perm, N_BLK))
    requester = jnp.arange(N_BLK, dtype=jnp.int32)[:, None]
    rank_ids = jnp.arange(entries, dtype=jnp.int32)[None, :]
    remote_count = jnp.minimum(entries, CAP * requester)
    offset = jax.random.randint(key_offset, (N_BLK, 1), 0, 1 << 20)
    owner_rank = jnp.where(rank_ids < remote_count, (offset + rank_ids // CAP) % jnp.maximum(requester, 1), requester)
    row_index = jnp.broadcast_to(requester, (N_BLK, entries))
    owner_slot = jnp.zeros((N_BLK, entries), jnp.int32).at[row_index, slot_order].set(owner_rank)
    slot_block = rank_ids // LIST
    query_id = requester * QB_DEV + slot_block
    remote_choice = owner_slot * QB_DEV + jax.random.randint(key_remote, (N_BLK, entries), 0, QB_DEV)
    local_draw = jax.random.randint(key_local, (N_BLK, entries), 0, 1 << 20)
    local_choice = jnp.where(slot_block > 0, requester * QB_DEV + local_draw % jnp.maximum(slot_block, 1), query_id)
    listed = jnp.where(owner_slot != requester, remote_choice, local_choice)
    listed = listed.reshape(TOKEN_BLOCKS, LIST).astype(jnp.int32)
    return listed.at[TOKEN_BLOCKS - 1, 0].set(TOKEN_BLOCKS - 1)


def plant(result, rng, low, top_value):
    shape = result.shape
    spot = [jax.random.randint(jax.random.fold_in(rng, axis), (), 0, shape[axis]) for axis in range(len(shape))]
    result = result.at[tuple(spot)].set(low)
    longest = shape.index(max(shape))
    spot[longest] = (spot[longest] + 1) % shape[longest]
    return result.at[tuple(spot)].set(top_value)


def steps_of(stream_key, shape, cuts, smallest, largest):
    level = 1.0
    for dim, blocks in cuts:
        heights = jax.random.uniform(jax.random.fold_in(jax.random.fold_in(stream_key, 6), dim), (blocks,), jnp.float32, smallest / len(cuts), largest / len(cuts))
        level = level * jnp.repeat(jnp.exp(heights), shape[dim] // blocks).reshape((-1,) + (1,) * (len(shape) - 1 - dim))
    return level


def bell_draw(rng, shape, scale, limit, cuts=(), kind=jnp.bfloat16):
    factor_of = steps_of(rng, shape, cuts, -0.22, 0.18) if cuts else 1.0
    values = jax.random.normal(rng, shape, jnp.float32) * scale * factor_of
    return jnp.minimum(jnp.maximum(values, -limit), limit).astype(kind)


def setup_inputs(seed: int = 0) -> dict:
    key_of = jax.random.split(jax.random.key(seed), 9)
    queries = draw_queries(jax.random.fold_in(key_of[8], 71), 0)
    key_state_rows = draw_key_state_rows(jax.random.fold_in(key_of[8], 71), 0)
    value_state_rows = bell_draw(key_of[2], (SEQUENCE_LENGTH, KEY_VALUE_HEADS * HEAD_SIZE), 1.0, 6.0, ((0, 256),))
    cotangent = bell_draw(key_of[3], (SEQUENCE_LENGTH, QUERY_HEAD_COUNT * HEAD_SIZE), 1.0, 6.0, ((0, 256),))
    block_list = draw_block_list(jax.random.fold_in(key_of[8], 71), 0)
    query_exponent = plant(jax.random.randint(key_of[5], (TOKEN_BLOCKS, QUERY_HEAD_COUNT), -5, 2), jax.random.fold_in(key_of[5], 1), -5, 1).astype(jnp.int32)
    key_block_exponent = plant(jax.random.randint(key_of[6], (TOKEN_BLOCKS, KEY_VALUE_HEADS), -5, 2), jax.random.fold_in(key_of[6], 1), -5, 1).astype(jnp.int32)
    value_block_exponent = plant(jax.random.randint(key_of[7], (TOKEN_BLOCKS, KEY_VALUE_HEADS), -5, 2), jax.random.fold_in(key_of[7], 1), -5, 1).astype(jnp.int32)
    return dict(queries=queries, key_state_rows=key_state_rows, value_state_rows=value_state_rows, cotangent=cotangent, block_list=block_list, query_exponent=query_exponent, key_block_exponent=key_block_exponent, value_block_exponent=value_block_exponent)


MAX_CODE = 448.0

def hadamard_table(order_n):
    indices = lax.iota(jnp.int32, order_n)
    common = jnp.bitwise_and(indices[:, None], indices[None, :])
    parity = jnp.zeros((order_n, order_n), jnp.int32)
    for bit_pos in range(order_n.bit_length() - 1):
        parity = parity + jnp.bitwise_and(jnp.right_shift(common, bit_pos), 1)
    return jnp.where(jnp.bitwise_and(parity, 1) == 0, 1.0, -1.0).astype(jnp.float32)

def quantize_rotated(states, exponent, hadamard_matrix):
    rotated = jnp.einsum('...d,de->...e', states.astype(jnp.float32), hadamard_matrix)
    factor = jnp.exp2(exponent.astype(jnp.float32))
    coded = jnp.clip(rotated / factor, -MAX_CODE, MAX_CODE).astype(jnp.bfloat16)
    coded = lax.optimization_barrier(coded)
    return (coded.astype(jnp.float32) * factor).astype(jnp.bfloat16)

def reference(queries, key_state_rows, value_state_rows, cotangent, block_list, query_exponent, key_block_exponent, value_block_exponent):
    copy_count = max(N_SP, KEY_VALUE_HEADS)
    repeat_count = copy_count // KEY_VALUE_HEADS
    per_copy = QUERY_HEAD_COUNT // copy_count
    hadamard_matrix = hadamard_table(HEAD_SIZE)
    score_scale = 1.0 / (HEAD_SIZE * math.sqrt(HEAD_SIZE))
    query_power = jnp.repeat(query_exponent, BLOCK, axis=0)[:, :, None]
    key_power_scale = jnp.repeat(key_block_exponent, BLOCK, axis=0)[:, :, None]
    value_power_scale = jnp.repeat(value_block_exponent, BLOCK, axis=0)[:, :, None]
    query_deq = quantize_rotated(queries.reshape(SEQUENCE_LENGTH, QUERY_HEAD_COUNT, HEAD_SIZE), query_power, hadamard_matrix).reshape(SEQUENCE_LENGTH, copy_count, per_copy, HEAD_SIZE)
    key_dequantized = jnp.repeat(quantize_rotated(key_state_rows.reshape(SEQUENCE_LENGTH, KEY_VALUE_HEADS, HEAD_SIZE), key_power_scale, hadamard_matrix), repeat_count, axis=1)
    value_dequantized = jnp.repeat(quantize_rotated(value_state_rows.reshape(SEQUENCE_LENGTH, KEY_VALUE_HEADS, HEAD_SIZE), value_power_scale, hadamard_matrix), repeat_count, axis=1)
    grad_rot = (jnp.einsum('thd,de->the', cotangent.reshape(SEQUENCE_LENGTH, QUERY_HEAD_COUNT, HEAD_SIZE).astype(jnp.float32), hadamard_matrix) / HEAD_SIZE).astype(jnp.bfloat16)
    grad_rot = grad_rot.reshape(SEQUENCE_LENGTH, copy_count, per_copy, HEAD_SIZE)
    causal = jnp.arange(BLOCK)[None, :] <= jnp.arange(BLOCK)[:, None]

    def one_block(block_index):
        row_start = block_index * BLOCK
        listed = block_list[block_index]
        key_blocks = jnp.concatenate([block_index[None], listed]).astype(jnp.int32)
        flags = []
        for entry in range(LIST):
            seen = jnp.zeros((), bool)
            for other in range(entry):
                seen = seen | (listed[other] == listed[entry])
            flags.append((listed[entry] != block_index) & jnp.logical_not(seen))
        entry_ok = jnp.stack(flags)
        key_rows = jnp.concatenate([lax.dynamic_slice_in_dim(key_dequantized, key_blocks[m] * BLOCK, BLOCK, 0) for m in range(1 + LIST)], axis=0)
        value_rows = jnp.concatenate([lax.dynamic_slice_in_dim(value_dequantized, key_blocks[m] * BLOCK, BLOCK, 0) for m in range(1 + LIST)], axis=0)
        allowed = jnp.concatenate([causal, jnp.broadcast_to(jnp.repeat(entry_ok, BLOCK)[None, :], (BLOCK, LIST * BLOCK))], axis=1)
        query_rows = lax.dynamic_slice_in_dim(query_deq, row_start, BLOCK, 0)
        grad_rows = lax.dynamic_slice_in_dim(grad_rot, row_start, BLOCK, 0)
        scores = jnp.einsum('qcgd,kcd->cgqk', query_rows.astype(jnp.float32), key_rows.astype(jnp.float32)) * score_scale
        masked = jnp.where(allowed[None, None], scores, -jnp.inf)
        row_max = lax.optimization_barrier(jnp.max(masked, axis=-1, keepdims=True))
        weights = jnp.exp(masked - row_max)
        probability = weights / lax.optimization_barrier(jnp.sum(weights, axis=-1, keepdims=True))
        probs_half = probability.astype(jnp.bfloat16)
        out_rot = jnp.einsum('cgqk,kcd->qcgd', probs_half.astype(jnp.float32), value_rows.astype(jnp.float32))
        attention_rows = (jnp.einsum('qcgd,de->qcge', out_rot, hadamard_matrix, precision=lax.Precision.HIGHEST) / HEAD_SIZE).astype(jnp.bfloat16)
        row_delta = jnp.transpose(lax.optimization_barrier(jnp.sum(grad_rows.astype(jnp.float32) * out_rot, axis=-1)), (1, 2, 0))
        prob_grad = jnp.einsum('qcgd,kcd->cgqk', grad_rows.astype(jnp.float32), value_rows.astype(jnp.float32))
        score_grad = probability * (prob_grad - row_delta[..., None])
        score_half = (score_grad * score_scale).astype(jnp.bfloat16)
        query_rot = jnp.einsum('cgqk,kcd->qcgd', score_half.astype(jnp.float32), key_rows.astype(jnp.float32))
        query_grad = jnp.einsum('qcgd,de->qcge', query_rot, hadamard_matrix, precision=lax.Precision.HIGHEST).astype(jnp.bfloat16)
        key_sums = jnp.einsum('cgqk,qcgd->kcd', score_half.astype(jnp.float32), query_rows.astype(jnp.float32))
        value_sums = jnp.einsum('cgqk,qcgd->kcd', probs_half.astype(jnp.float32), grad_rows.astype(jnp.float32))
        pair_sums = jnp.stack([key_sums, value_sums], axis=2).reshape(1 + LIST, BLOCK, copy_count, 2, HEAD_SIZE)
        return (attention_rows.reshape(BLOCK, QUERY_HEAD_COUNT * HEAD_SIZE), query_grad.reshape(BLOCK, QUERY_HEAD_COUNT * HEAD_SIZE), pair_sums[0], pair_sums[1:].astype(jnp.bfloat16))
    attention, query_gradient_rows, diagonal, entry_partials = lax.map(one_block, jnp.arange(TOKEN_BLOCKS, dtype=jnp.int32))
    targets = block_list.reshape(-1).astype(jnp.int32)
    pair_rot = diagonal.at[targets].add(entry_partials.reshape(TOKEN_BLOCKS * LIST, BLOCK, copy_count, 2, HEAD_SIZE).astype(jnp.float32))
    pair_duplicate = jnp.einsum('...d,de->...e', pair_rot, hadamard_matrix, precision=lax.Precision.HIGHEST).astype(jnp.bfloat16)
    summed_rows = lax.optimization_barrier(jnp.sum(pair_duplicate.astype(jnp.float32).reshape(SEQUENCE_LENGTH, KEY_VALUE_HEADS, repeat_count, 2, HEAD_SIZE), axis=2)).astype(jnp.bfloat16)
    return (attention.reshape(SEQUENCE_LENGTH, QUERY_HEAD_COUNT * HEAD_SIZE), query_gradient_rows.reshape(SEQUENCE_LENGTH, QUERY_HEAD_COUNT * HEAD_SIZE), summed_rows[:, :, 0].reshape(SEQUENCE_LENGTH, KEY_VALUE_HEADS * HEAD_SIZE), summed_rows[:, :, 1].reshape(SEQUENCE_LENGTH, KEY_VALUE_HEADS * HEAD_SIZE))
```

```python
import math

import jax
import jax.numpy as jnp
import numpy as np
from jax import lax
from jax.experimental import pallas as pl
from jax.experimental.pallas import tpu as pltpu
from jax.sharding import PartitionSpec as P

QUERY_HEAD_COUNT = 64
KEY_VALUE_HEADS = 8
HEAD_SIZE = 128
BLOCK = 128
CAP = 2
GROUP = QUERY_HEAD_COUNT // KEY_VALUE_HEADS
ROWS = GROUP * BLOCK
SLICES = 2 * KEY_VALUE_HEADS
MAX_CODE = 448.0
SCORE_SCALE = 1.0 / (HEAD_SIZE * math.sqrt(HEAD_SIZE))
BF16 = jnp.bfloat16
F32 = jnp.float32
VMEM_LIMIT = 48 * 1024 * 1024


def hadamard_table():
    index = np.arange(HEAD_SIZE)
    common = index[:, None] & index[None, :]
    parity = np.zeros_like(common)
    for bit in range(HEAD_SIZE.bit_length() - 1):
        parity += (common >> bit) & 1
    return np.where(parity % 2 == 0, 1.0, -1.0).astype(jnp.bfloat16)


def matmul(a, b):
    return lax.dot_general(a, b, (((1,), (0,)), ((), ())), preferred_element_type=F32)


def matmul_nt(a, b):
    return lax.dot_general(a, b, (((1,), (1,)), ((), ())), preferred_element_type=F32)


def matmul_tn(a, b):
    return lax.dot_general(a, b, (((0,), (0,)), ((), ())), preferred_element_type=F32)


def quantize(states, hadamard, inverse, factor):
    coded = jnp.clip(matmul(states, hadamard) * inverse, -MAX_CODE, MAX_CODE).astype(BF16)
    return (coded.astype(F32) * factor).astype(BF16)


def lanes(ref, head):
    return ref[:, head * HEAD_SIZE : (head + 1) * HEAD_SIZE]


def stack_heads(ref):
    return jnp.concatenate([lanes(ref, head) for head in range(GROUP)], axis=0)


def pack_kernel(factors, hadamard_ref, key_ref, value_ref, out_ref):
    hadamard = hadamard_ref[...]
    for head in range(KEY_VALUE_HEADS):
        out_ref[2 * head] = quantize(lanes(key_ref, head), hadamard, factors[0, head], factors[1, head])
        value = quantize(lanes(value_ref, head), hadamard, factors[2, head], factors[3, head])
        out_ref[2 * head + 1] = (matmul(value, hadamard) * (1.0 / HEAD_SIZE)).astype(BF16)


def pick_kernel(index, source_ref, out_ref):
    for slot in range(out_ref.shape[0]):
        out_ref[slot] = source_ref[index[slot]]


def pick_entries_kernel(index, own_ref, remote_ref, out_ref):
    count = own_ref.shape[0]
    for slot in range(out_ref.shape[0]):
        place = index[slot]

        @pl.when(place < count)
        def _():
            out_ref[slot] = own_ref[jnp.minimum(place, count - 1)]

        @pl.when(place >= count)
        def _():
            out_ref[slot] = remote_ref[jnp.maximum(place - count, 0)]


def accumulate_kernel(index, own_ref, remote_ref, out_ref, total):
    total[...] = jnp.zeros_like(total)
    count = own_ref.shape[0]
    for slot in range(count):
        place = index[slot]
        total[place] += own_ref[slot].astype(F32)
    for slot in range(remote_ref.shape[0]):
        place = index[count + slot]
        total[place] += remote_ref[slot].astype(F32)
    out_ref[...] = total[: out_ref.shape[0]].astype(BF16)


def finish_kernel(own_ref, listed_ref, key_ref, value_ref):
    for head in range(KEY_VALUE_HEADS):
        cols = slice(head * HEAD_SIZE, (head + 1) * HEAD_SIZE)
        total = own_ref[2 * head : 2 * head + 2] + listed_ref[2 * head : 2 * head + 2].astype(F32)
        key_ref[:, cols] = total[0].astype(BF16)
        value_ref[:, cols] = total[1].astype(BF16)


def causal_mask():
    keys = lax.broadcasted_iota(jnp.int32, (BLOCK, ROWS), 0)
    queries = lax.broadcasted_iota(jnp.int32, (BLOCK, ROWS), 1) % BLOCK
    return keys <= queries


def own_kernel(factors, hadamard_ref, query_ref, grad_ref, pair_ref, deq_ref, stats_ref):
    group = pl.program_id(0)
    hadamard = hadamard_ref[...]
    for head in range(GROUP):
        place = group * GROUP + head
        deq_ref[0, head * BLOCK : (head + 1) * BLOCK, :] = quantize(
            lanes(query_ref, head), hadamard, factors[0, place], factors[1, place]
        )
    scores = matmul_nt(pair_ref[0], deq_ref[0]) * SCORE_SCALE
    scores = jnp.where(causal_mask(), scores, -jnp.inf)
    top = jnp.max(scores, axis=0, keepdims=True)
    weights = jnp.exp(scores - top)
    prob_grad = matmul_nt(pair_ref[1], stack_heads(grad_ref))
    stats_ref[0, 0:1, :] = top
    stats_ref[0, 1:2, :] = jnp.sum(weights, axis=0, keepdims=True)
    stats_ref[0, 2:3, :] = jnp.sum(weights * prob_grad, axis=0, keepdims=True)


def listed_kernel(
    valid, hadamard_ref, deq_ref, grad_ref, pair_ref, stats_ref, pair_out, final_ref
):
    deq = deq_ref[0]
    grad = stack_heads(grad_ref)
    scores = matmul_nt(pair_ref[0], deq) * SCORE_SCALE
    scores = jnp.where(valid[0] > 0, scores, -jnp.inf)
    own_top = stats_ref[0, 0:1, :]
    top = jnp.maximum(own_top, jnp.max(scores, axis=0, keepdims=True))
    weights = jnp.exp(scores - top)
    shrink = jnp.exp(own_top - top)
    inverse = 1.0 / (stats_ref[0, 1:2, :] * shrink + jnp.sum(weights, axis=0, keepdims=True))
    prob_grad = matmul_nt(pair_ref[1], grad)
    delta = stats_ref[0, 2:3, :] * shrink + jnp.sum(weights * prob_grad, axis=0, keepdims=True)
    delta = delta * inverse
    probs = weights * inverse
    score_grad = (probs * (prob_grad - delta) * SCORE_SCALE).astype(BF16)
    key_sum = matmul(score_grad, deq).astype(BF16)
    pair_out[0] = matmul(key_sum, hadamard_ref[...]).astype(BF16)
    pair_out[1] = matmul(probs.astype(BF16), grad).astype(BF16)
    final_ref[0, 0:1, :] = top
    final_ref[0, 1:2, :] = inverse
    final_ref[0, 2:3, :] = delta


def finish_rows(array, out_ref):
    for head in range(GROUP):
        cols = slice(head * HEAD_SIZE, (head + 1) * HEAD_SIZE)
        out_ref[:, cols] = array[head * BLOCK : (head + 1) * BLOCK].astype(BF16)


def rest_kernel(
    valid,
    hadamard_ref,
    deq_ref,
    grad_ref,
    own_ref,
    listed_ref,
    final_ref,
    attention_ref,
    query_grad_ref,
    pair_out,
):
    hadamard = hadamard_ref[...]
    deq = deq_ref[0]
    grad = stack_heads(grad_ref)
    top = final_ref[0, 0:1, :]
    inverse = final_ref[0, 1:2, :]
    delta = final_ref[0, 2:3, :]

    def part(key, value, mask):
        scores = matmul_nt(key, deq) * SCORE_SCALE
        probs = jnp.exp(jnp.where(mask, scores, -jnp.inf) - top) * inverse
        prob_grad = matmul_nt(value, grad)
        score_grad = (probs * (prob_grad - delta) * SCORE_SCALE).astype(BF16)
        return probs.astype(BF16), score_grad

    own_probs, own_score = part(own_ref[0], own_ref[1], causal_mask())
    listed_probs, listed_score = part(listed_ref[0], listed_ref[1], valid[0] > 0)
    pair_out[0] = matmul(matmul(own_score, deq).astype(BF16), hadamard)
    pair_out[1] = matmul(own_probs, grad)
    keys = jnp.concatenate([own_ref[0], listed_ref[0]], axis=0)
    keys = matmul(keys, hadamard).astype(BF16)
    values = jnp.concatenate([own_ref[1], listed_ref[1]], axis=0)
    finish_rows(matmul_tn(jnp.concatenate([own_probs, listed_probs], axis=0), values), attention_ref)
    finish_rows(matmul_tn(jnp.concatenate([own_score, listed_score], axis=0), keys), query_grad_ref)


def params():
    return pltpu.CompilerParams(vmem_limit_bytes=VMEM_LIMIT)


def smem():
    return pl.BlockSpec(memory_space=pltpu.SMEM)


def vmem():
    return pl.BlockSpec(memory_space=pltpu.VMEM)


def shape(*dims, dtype=BF16):
    return jax.ShapeDtypeStruct(dims, dtype)


def pick(index, source):
    count = index.shape[0]
    return pl.pallas_call(
        pick_kernel,
        out_shape=shape(count, *source.shape[1:]),
        in_specs=[smem(), vmem()],
        out_specs=vmem(),
        compiler_params=params(),
        name="pick",
    )(index, source)


def pick_entries(index, own, remote):
    count = index.shape[0]
    return pl.pallas_call(
        pick_entries_kernel,
        out_shape=shape(count, *own.shape[1:]),
        in_specs=[smem(), vmem(), vmem()],
        out_specs=vmem(),
        compiler_params=params(),
        name="pick_entries",
    )(index, own, remote)


def accumulate(index, own, remote):
    return pl.pallas_call(
        accumulate_kernel,
        out_shape=shape(*own.shape),
        in_specs=[smem(), vmem(), vmem()],
        out_specs=vmem(),
        scratch_shapes=[pltpu.VMEM((own.shape[0] + 1, *own.shape[1:]), F32)],
        compiler_params=params(),
        name="accumulate",
    )(index, own, remote)


def pack(factors, hadamard, keys, values):
    return pl.pallas_call(
        pack_kernel,
        out_shape=shape(SLICES, BLOCK, HEAD_SIZE),
        in_specs=[smem(), vmem(), vmem(), vmem()],
        out_specs=vmem(),
        compiler_params=params(),
        name="pack",
    )(factors, hadamard, keys, values)


def finish(own, listed):
    out = shape(BLOCK, KEY_VALUE_HEADS * HEAD_SIZE)
    return pl.pallas_call(
        finish_kernel,
        out_shape=(out, out),
        in_specs=[vmem(), vmem()],
        out_specs=(vmem(), vmem()),
        compiler_params=params(),
        name="finish",
    )(own, listed)


HADAMARD = pl.BlockSpec((HEAD_SIZE, HEAD_SIZE), lambda m: (0, 0))
TOKENS = pl.BlockSpec((BLOCK, ROWS), lambda m: (0, m))
STACKED = pl.BlockSpec((1, ROWS, HEAD_SIZE), lambda m: (m, 0, 0))
PAIR = pl.BlockSpec((2, BLOCK, HEAD_SIZE), lambda m: (m, 0, 0))
STATS = pl.BlockSpec((1, 8, ROWS), lambda m: (m, 0, 0))
STATS_SHAPE = shape(KEY_VALUE_HEADS, 8, ROWS, dtype=F32)
UNIT = 2 * BLOCK * ROWS * HEAD_SIZE * KEY_VALUE_HEADS


def cost(units, megabytes):
    return pl.CostEstimate(
        flops=units * UNIT, bytes_accessed=megabytes << 20, transcendentals=BLOCK * ROWS * KEY_VALUE_HEADS
    )


def own_part(factors, hadamard, queries, cotangent, packed):
    return pl.pallas_call(
        own_kernel,
        grid=(KEY_VALUE_HEADS,),
        out_shape=(shape(KEY_VALUE_HEADS, ROWS, HEAD_SIZE), STATS_SHAPE),
        in_specs=[smem(), HADAMARD, TOKENS, TOKENS, PAIR],
        out_specs=(STACKED, STATS),
        compiler_params=params(),
        cost_estimate=cost(3, 7),
        name="own_part",
    )(factors, hadamard, queries, cotangent, packed)


def listed_part(valid, hadamard, deq, cotangent, listed, stats):
    return pl.pallas_call(
        listed_kernel,
        grid=(KEY_VALUE_HEADS,),
        out_shape=(shape(SLICES, BLOCK, HEAD_SIZE), STATS_SHAPE),
        in_specs=[smem(), HADAMARD, STACKED, TOKENS, PAIR, STATS],
        out_specs=(PAIR, STATS),
        compiler_params=params(),
        cost_estimate=cost(4, 6),
        name="listed_part",
    )(valid, hadamard, deq, cotangent, listed, stats)


def rest_part(valid, hadamard, deq, cotangent, packed, listed, final):
    rows = shape(BLOCK, QUERY_HEAD_COUNT * HEAD_SIZE)
    sums = shape(SLICES, BLOCK, HEAD_SIZE, dtype=F32)
    return pl.pallas_call(
        rest_kernel,
        grid=(KEY_VALUE_HEADS,),
        out_shape=(rows, rows, sums),
        in_specs=[smem(), HADAMARD, STACKED, TOKENS, PAIR, PAIR, STATS],
        out_specs=(TOKENS, TOKENS, PAIR),
        compiler_params=params(),
        cost_estimate=cost(10, 11),
        name="rest_part",
    )(valid, hadamard, deq, cotangent, packed, listed, final)


def exchange(array, axis):
    return lax.all_to_all(array, axis, split_axis=0, concat_axis=0, tiled=True)


def powers(exponent):
    up = (jnp.left_shift(1, exponent + 5)).astype(F32) * (1.0 / 32.0)
    down = (jnp.left_shift(1, 1 - exponent)).astype(F32) * 0.5
    return down, up


def local(
    queries,
    key_state_rows,
    value_state_rows,
    cotangent,
    block_list,
    query_exponent,
    key_block_exponent,
    value_block_exponent,
):
    sp_count = lax.axis_size("sp")
    blk_count = lax.axis_size("blk")
    sp_index = lax.axis_index("sp")
    blk_index = lax.axis_index("blk")
    hadamard = jnp.asarray(hadamard_table())

    def own_row(table):
        return lax.dynamic_index_in_dim(table, sp_index, 0, keepdims=False)

    query_factors = jnp.stack(powers(own_row(query_exponent)))
    pair_factors = jnp.stack(
        powers(own_row(key_block_exponent)) + powers(own_row(value_block_exponent))
    )

    listed = block_list.reshape(blk_count, sp_count)
    owners = listed // sp_count
    slots = jnp.arange(sp_count, dtype=jnp.int32)
    caps = jnp.arange(CAP, dtype=jnp.int32)
    groups = jnp.arange(blk_count, dtype=jnp.int32)
    remote = owners != groups[:, None]
    before = (
        (owners[:, :, None] == owners[:, None, :])
        & remote[:, None, :]
        & (slots[None, None, :] < slots[None, :, None])
    )
    rank = jnp.minimum(jnp.sum(before.astype(jnp.int32), axis=2), CAP - 1)
    serves = (
        remote[:, None, :]
        & (owners[:, None, :] == blk_index)
        & (rank[:, None, :] == caps[None, :, None])
    )
    serve_any = jnp.any(serves, axis=2).reshape(-1)
    serve_block = jnp.sum(jnp.where(serves, listed[:, None, :] % sp_count, 0), axis=2).reshape(-1)
    serve_block = jnp.clip(serve_block, 0, sp_count - 1)
    serve_target = jnp.where(serve_any, serve_block, sp_count)

    def own_group(table):
        return lax.dynamic_index_in_dim(table, blk_index, 0, keepdims=False)

    my_listed, my_owner, my_rank, my_remote = (
        own_group(listed),
        own_group(owners),
        own_group(rank),
        own_group(remote),
    )
    my_place = my_listed % sp_count
    entry_place = jnp.where(my_remote, sp_count + my_owner * CAP + my_rank, my_place)
    back = (
        my_remote[None, None, :]
        & (my_owner[None, None, :] == groups[:, None, None])
        & (my_rank[None, None, :] == caps[None, :, None])
    )
    back_entry = jnp.sum(jnp.where(back, slots[None, None, :], 0), axis=2).reshape(-1)
    back_entry = jnp.clip(back_entry, 0, sp_count - 1)
    entry_target = jnp.where(my_remote, sp_count, my_place)
    targets = jnp.concatenate([entry_target, serve_target])
    own_block = blk_index * sp_count + sp_index
    valid = (own_row(my_listed) != own_block).astype(jnp.int32).reshape(1)

    packed = pack(pair_factors, hadamard, key_state_rows, value_state_rows)
    slices = exchange(packed, "sp")
    outgoing, own_pairs = lax.optimization_barrier((pick(serve_block, slices), packed))
    arrived = exchange(outgoing.reshape(blk_count, CAP, BLOCK, HEAD_SIZE), "blk")
    arrived = arrived.reshape(blk_count * CAP, BLOCK, HEAD_SIZE)
    own = own_part(query_factors, hadamard, queries, cotangent, own_pairs)
    arrived, deq, stats = lax.optimization_barrier((arrived, *own))
    entries = exchange(pick_entries(entry_place, slices, arrived), "sp")
    entry_pairs, final = listed_part(valid, hadamard, deq, cotangent, entries, stats)
    entry_grads = exchange(entry_pairs, "sp")
    returning, final = lax.optimization_barrier((pick(back_entry, entry_grads), final))
    returned = exchange(returning.reshape(blk_count, CAP, BLOCK, HEAD_SIZE), "blk")
    returned = returned.reshape(blk_count * CAP, BLOCK, HEAD_SIZE)
    rest = rest_part(valid, hadamard, deq, cotangent, packed, entries, final)
    returned, attention, query_grad, own_sums = lax.optimization_barrier((returned, *rest))
    sums = exchange(accumulate(targets, entry_grads, returned), "sp")
    key_grad, value_grad = finish(own_sums, sums)
    return attention, query_grad, key_grad, value_grad


def solution(mesh):
    rows = P(("blk", "sp"), None)
    return jax.shard_map(
        local,
        mesh=mesh,
        in_specs=(rows, rows, rows, rows, P(), P("blk", None), P("blk", None), P("blk", None)),
        out_specs=(rows, rows, rows, rows),
        check_vma=False,
    )
```

```python
import math

import jax
import jax.numpy as jnp
import numpy as np
from jax import lax
from jax.experimental import pallas as pl
from jax.experimental.pallas import tpu as pltpu
from jax.sharding import PartitionSpec as P

QUERY_HEAD_COUNT = 64
KEY_VALUE_HEADS = 8
HEAD_SIZE = 128
BLOCK = 128
GROUP = QUERY_HEAD_COUNT // KEY_VALUE_HEADS
ROWS = GROUP * BLOCK
SLICES = 2 * KEY_VALUE_HEADS
PIECE = 8
MAX_CODE = 448.0
SCORE_SCALE = 1.0 / (HEAD_SIZE * math.sqrt(HEAD_SIZE))
BF16 = jnp.bfloat16
F32 = jnp.float32
CHUNK = 256
UNROLL = 16


def hadamard_table():
    index = np.arange(HEAD_SIZE)
    common = index[:, None] & index[None, :]
    parity = np.zeros_like(common)
    for bit in range(HEAD_SIZE.bit_length() - 1):
        parity += (common >> bit) & 1
    return np.where(parity % 2 == 0, 1.0, -1.0).astype(jnp.bfloat16)


def matmul(a, b):
    return lax.dot_general(a, b, (((1,), (0,)), ((), ())), preferred_element_type=F32)


def matmul_nt(a, b):
    return lax.dot_general(a, b, (((1,), (1,)), ((), ())), preferred_element_type=F32)


def matmul_tn(a, b):
    return lax.dot_general(a, b, (((0,), (0,)), ((), ())), preferred_element_type=F32)


def quantize(states, hadamard, inverse, factor):
    coded = jnp.clip(matmul(states, hadamard) * inverse, -MAX_CODE, MAX_CODE).astype(BF16)
    return (coded.astype(F32) * factor).astype(BF16)


def lanes(ref, head):
    return ref[:, head * HEAD_SIZE : (head + 1) * HEAD_SIZE]


def stack_heads(ref):
    return jnp.concatenate([lanes(ref, head) for head in range(GROUP)], axis=0)


def power(exponent, shift, scale):
    return jnp.left_shift(jnp.ones_like(exponent), exponent + shift).astype(F32) * scale


def own_powers(table, row):
    blocks = lax.broadcasted_iota(jnp.int32, table.shape, 1)
    level = jnp.sum(jnp.where(blocks == row, table, 0), axis=1, keepdims=True)
    return power(-level, 1, 0.5), power(level, 5, 1.0 / 32.0)


def pack_kernel(key_exponent, value_exponent, hadamard_ref, key_ref, value_ref, out_ref):
    hadamard = hadamard_ref[...]
    row = lax.axis_index("sp")

    def coded(ref, exponent_ref):
        stacked = jnp.concatenate([lanes(ref, head) for head in range(KEY_VALUE_HEADS)], axis=0)
        rotated = matmul(stacked, hadamard)
        down, up = own_powers(exponent_ref[...], row)
        parts = []
        for head in range(KEY_VALUE_HEADS):
            one = slice(head, head + 1)
            part = rotated[head * BLOCK : (head + 1) * BLOCK] * down[one, :]
            part = jnp.clip(part, -MAX_CODE, MAX_CODE).astype(BF16)
            parts.append((part.astype(F32) * up[one, :]).astype(BF16))
        return parts

    keys = coded(key_ref, key_exponent)
    values = matmul(jnp.concatenate(coded(value_ref, value_exponent), axis=0), hadamard)
    values = (values * (1.0 / HEAD_SIZE)).astype(BF16)
    for head in range(KEY_VALUE_HEADS):
        out_ref[2 * head] = keys[head]
        out_ref[2 * head + 1] = values[head * BLOCK : (head + 1) * BLOCK]


def pick_kernel(index, source_ref, out_ref):
    def some(step, carry):
        for place in range(UNROLL):
            row = step * UNROLL + place
            out_ref[row] = source_ref[index[row]]
        return carry

    lax.fori_loop(0, out_ref.shape[0] // UNROLL, some, 0)


def accumulate_kernel(index, part_ref, out_ref, even, odd):
    even[...] = jnp.zeros_like(even)
    odd[...] = jnp.zeros_like(odd)

    def some(step, carry):
        for place in range(UNROLL):
            row = step * UNROLL + place
            total = even if place % 2 == 0 else odd
            total[index[row]] += part_ref[row].astype(F32)
        return carry

    lax.fori_loop(0, part_ref.shape[0] // UNROLL, some, 0)
    out_ref[...] = (even[...] + odd[...]).astype(BF16)


def finish_kernel(own_ref, listed_ref, key_ref, value_ref):
    for head in range(KEY_VALUE_HEADS):
        cols = slice(head * HEAD_SIZE, (head + 1) * HEAD_SIZE)
        total = own_ref[2 * head : 2 * head + 2] + listed_ref[2 * head : 2 * head + 2].astype(F32)
        key_ref[:, cols] = total[0].astype(BF16)
        value_ref[:, cols] = total[1].astype(BF16)


def causal_mask():
    keys = lax.broadcasted_iota(jnp.int32, (BLOCK, ROWS), 0)
    queries = lax.broadcasted_iota(jnp.int32, (BLOCK, ROWS), 1) % BLOCK
    return keys <= queries


def own_kernel(exponent, hadamard_ref, query_ref, grad_ref, pair_ref, deq_ref, stats_ref):
    group = pl.program_id(0)
    hadamard = hadamard_ref[...]
    row = lax.axis_index("sp")
    for head in range(GROUP):
        level = exponent[row, group * GROUP + head]
        deq_ref[0, head * BLOCK : (head + 1) * BLOCK, :] = quantize(
            lanes(query_ref, head), hadamard, power(-level, 1, 0.5), power(level, 5, 1.0 / 32.0)
        )
    scores = matmul_nt(pair_ref[0], deq_ref[0]) * SCORE_SCALE
    scores = jnp.where(causal_mask(), scores, -jnp.inf)
    top = jnp.max(scores, axis=0, keepdims=True)
    weights = jnp.exp(scores - top)
    prob_grad = matmul_nt(pair_ref[1], stack_heads(grad_ref))
    stats_ref[0, 0:1, :] = top
    stats_ref[0, 1:2, :] = jnp.sum(weights, axis=0, keepdims=True)
    stats_ref[0, 2:3, :] = jnp.sum(weights * prob_grad, axis=0, keepdims=True)


def own_block():
    return lax.axis_index("blk") * lax.axis_size("sp") + lax.axis_index("sp")


def lists_other(index):
    block = own_block()
    return index[block] != block


def listed_kernel(
    index, hadamard_ref, deq_ref, grad_ref, pair_ref, stats_ref, pair_out, final_ref, score_scr, prob_scr
):
    listed = lists_other(index)

    def softmax(head, slot, start):
        cols = slice(start, start + CHUNK)
        grad = grad_rows(head, start // BLOCK, CHUNK // BLOCK)
        scores = matmul_nt(pair_ref[2 * head], deq_ref[head, cols, :])
        prob_grad = matmul_nt(pair_ref[2 * head + 1], grad)
        own_top = stats_ref[head, 0:1, cols]
        best = jnp.max(scores, axis=0, keepdims=True) * SCORE_SCALE
        top = jnp.maximum(own_top, jnp.where(listed, best, -jnp.inf))
        weights = jnp.exp(scores * SCORE_SCALE - jnp.where(listed, top, jnp.inf))
        shrink = jnp.exp(own_top - top)
        inverse = 1.0 / (
            stats_ref[head, 1:2, cols] * shrink + jnp.sum(weights, axis=0, keepdims=True)
        )
        delta = stats_ref[head, 2:3, cols] * shrink
        delta = (delta + jnp.sum(weights * prob_grad, axis=0, keepdims=True)) * inverse
        scaled = inverse * SCORE_SCALE
        prob_scr[slot, :, cols] = (weights * inverse).astype(BF16)
        score_scr[slot, :, cols] = (weights * (prob_grad * scaled - delta * scaled)).astype(BF16)
        final_ref[head, 0:1, cols] = top
        final_ref[head, 1:2, cols] = inverse
        final_ref[head, 2:3, cols] = delta

    def grad_rows(head, first, count):
        return jnp.concatenate(
            [lanes(grad_ref, head * GROUP + first + place) for place in range(count)], axis=0
        )

    for head in range(KEY_VALUE_HEADS + 1):
        if head < KEY_VALUE_HEADS:
            for start in range(0, ROWS, CHUNK):
                softmax(head, head % 2, start)
        if head > 0:
            last, slot = head - 1, (head - 1) % 2
            key_sum = matmul(score_scr[slot], deq_ref[last]).astype(BF16)
            pair_out[2 * last] = matmul(key_sum, hadamard_ref[...]).astype(BF16)
            value_sum = matmul(prob_scr[slot], grad_rows(last, 0, GROUP))
            pair_out[2 * last + 1] = value_sum.astype(BF16)


def finish_rows(array, out_ref):
    for head in range(GROUP):
        cols = slice(head * HEAD_SIZE, (head + 1) * HEAD_SIZE)
        out_ref[:, cols] = array[head * BLOCK : (head + 1) * BLOCK].astype(BF16)


def rest_kernel(
    index,
    hadamard_ref,
    deq_ref,
    grad_ref,
    own_ref,
    listed_ref,
    final_ref,
    attention_ref,
    query_grad_ref,
    pair_out,
):
    hadamard = hadamard_ref[...]
    deq = deq_ref[0]
    grad = stack_heads(grad_ref)
    top = final_ref[0, 0:1, :]
    inverse = final_ref[0, 1:2, :]
    delta = final_ref[0, 2:3, :]

    def part(key, value, mask):
        scores = matmul_nt(key, deq) * SCORE_SCALE
        probs = jnp.exp(jnp.where(mask, scores, -jnp.inf) - top) * inverse
        prob_grad = matmul_nt(value, grad)
        score_grad = (probs * (prob_grad - delta) * SCORE_SCALE).astype(BF16)
        return probs.astype(BF16), score_grad

    own_probs, own_score = part(own_ref[0], own_ref[1], causal_mask())
    listed_probs, listed_score = part(listed_ref[0], listed_ref[1], lists_other(index))
    pair_out[0] = matmul(matmul(own_score, deq).astype(BF16), hadamard)
    pair_out[1] = matmul(own_probs, grad)
    keys = jnp.concatenate([own_ref[0], listed_ref[0]], axis=0)
    keys = matmul(keys, hadamard).astype(BF16)
    values = jnp.concatenate([own_ref[1], listed_ref[1]], axis=0)
    finish_rows(matmul_tn(jnp.concatenate([own_probs, listed_probs], axis=0), values), attention_ref)
    finish_rows(matmul_tn(jnp.concatenate([own_score, listed_score], axis=0), keys), query_grad_ref)


def params(megabytes=16):
    return pltpu.CompilerParams(vmem_limit_bytes=megabytes << 20)


def smem():
    return pl.BlockSpec(memory_space=pltpu.SMEM)


def vmem():
    return pl.BlockSpec(memory_space=pltpu.VMEM)


def hbm():
    return pl.BlockSpec(memory_space=pltpu.HBM)


def shape(*dims, dtype=BF16):
    return jax.ShapeDtypeStruct(dims, dtype)


def pick(index, source):
    return pl.pallas_call(
        pick_kernel,
        out_shape=shape(*source.shape),
        in_specs=[smem(), vmem()],
        out_specs=vmem(),
        compiler_params=params(),
        name="pick",
    )(index, source)


def accumulate(index, parts):
    return pl.pallas_call(
        accumulate_kernel,
        out_shape=shape(*parts.shape),
        in_specs=[smem(), vmem()],
        out_specs=vmem(),
        scratch_shapes=[pltpu.VMEM(parts.shape, F32)] * 2,
        compiler_params=params(),
        name="accumulate",
    )(index, parts)


def pack(key_exponent, value_exponent, hadamard, keys, values):
    return pl.pallas_call(
        pack_kernel,
        out_shape=shape(SLICES, BLOCK, HEAD_SIZE),
        in_specs=[vmem()] * 5,
        out_specs=vmem(),
        compiler_params=params(60),
        name="pack",
    )(key_exponent, value_exponent, hadamard, keys, values)


def finish(own, listed):
    out = shape(BLOCK, KEY_VALUE_HEADS * HEAD_SIZE)
    return pl.pallas_call(
        finish_kernel,
        out_shape=(out, out),
        in_specs=[vmem(), vmem()],
        out_specs=(vmem(), vmem()),
        compiler_params=params(),
        name="finish",
    )(own, listed)


HADAMARD = pl.BlockSpec((HEAD_SIZE, HEAD_SIZE), lambda m: (0, 0))
TOKENS = pl.BlockSpec((BLOCK, ROWS), lambda m: (0, m))
STACKED = pl.BlockSpec((1, ROWS, HEAD_SIZE), lambda m: (m, 0, 0))
PAIR = pl.BlockSpec((2, BLOCK, HEAD_SIZE), lambda m: (m, 0, 0))
STATS = pl.BlockSpec((1, 8, ROWS), lambda m: (m, 0, 0))
STATS_SHAPE = shape(KEY_VALUE_HEADS, 8, ROWS, dtype=F32)
UNIT = 2 * BLOCK * ROWS * HEAD_SIZE * KEY_VALUE_HEADS


def cost(units, megabytes):
    return pl.CostEstimate(
        flops=units * UNIT, bytes_accessed=megabytes << 20, transcendentals=BLOCK * ROWS * KEY_VALUE_HEADS
    )


def own_part(exponent, hadamard, queries, cotangent, packed):
    return pl.pallas_call(
        own_kernel,
        grid=(KEY_VALUE_HEADS,),
        out_shape=(shape(KEY_VALUE_HEADS, ROWS, HEAD_SIZE), STATS_SHAPE),
        in_specs=[smem(), HADAMARD, TOKENS, TOKENS, PAIR],
        out_specs=(STACKED, STATS),
        compiler_params=params(),
        cost_estimate=cost(3, 7),
        name="own_part",
    )(exponent, hadamard, queries, cotangent, packed)


def listed_part(index, hadamard, deq, cotangent, listed, stats):
    return pl.pallas_call(
        listed_kernel,
        out_shape=(shape(SLICES, BLOCK, HEAD_SIZE), STATS_SHAPE),
        in_specs=[smem()] + [vmem()] * 5,
        out_specs=(vmem(), vmem()),
        scratch_shapes=[pltpu.VMEM((2, BLOCK, ROWS), BF16)] * 2,
        compiler_params=params(),
        cost_estimate=cost(4, 6),
        name="listed_part",
    )(index, hadamard, deq, cotangent, listed, stats)


def rest_part(index, hadamard, deq, cotangent, packed, listed, final):
    rows = shape(BLOCK, QUERY_HEAD_COUNT * HEAD_SIZE)
    sums = shape(SLICES, BLOCK, HEAD_SIZE, dtype=F32)
    return pl.pallas_call(
        rest_kernel,
        grid=(KEY_VALUE_HEADS,),
        out_shape=(rows, rows, sums),
        in_specs=[smem(), HADAMARD, STACKED, TOKENS, PAIR, PAIR, STATS],
        out_specs=(TOKENS, TOKENS, PAIR),
        compiler_params=params(),
        cost_estimate=cost(10, 11),
        name="rest_part",
    )(index, hadamard, deq, cotangent, packed, listed, final)


def exchange(array):
    pieces = array.reshape(-1, PIECE, HEAD_SIZE)
    return lax.all_to_all(pieces, ("blk", "sp"), split_axis=0, concat_axis=0, tiled=True)


def whole(pieces):
    return pieces.reshape(SLICES, BLOCK, HEAD_SIZE)


def local(
    queries,
    key_state_rows,
    value_state_rows,
    cotangent,
    block_list,
    query_exponent,
    key_block_exponent,
    value_block_exponent,
):
    hadamard = jnp.asarray(hadamard_table())
    index = block_list.reshape(-1)
    packed = pack(
        key_block_exponent.T, value_block_exponent.T, hadamard, key_state_rows, value_state_rows
    )
    pieces = exchange(packed)
    own = own_part(query_exponent, hadamard, queries, cotangent, packed)
    pieces, deq, stats = lax.optimization_barrier((pieces, *own))
    entries = whole(exchange(pick(index, pieces)))
    entry_pairs, final = listed_part(index, hadamard, deq, cotangent, entries, stats)
    parts = exchange(entry_pairs)
    rest = rest_part(index, hadamard, deq, cotangent, packed, entries, final)
    parts, attention, query_grad, own_sums = lax.optimization_barrier((parts, *rest))
    sums = whole(exchange(accumulate(index, parts)))
    key_grad, value_grad = finish(own_sums, sums)
    return attention, query_grad, key_grad, value_grad


def solution(mesh):
    rows = P(("blk", "sp"), None)
    return jax.shard_map(
        local,
        mesh=mesh,
        in_specs=(rows, rows, rows, rows, P(), P("blk", None), P("blk", None), P("blk", None)),
        out_specs=(rows, rows, rows, rows),
        check_vma=False,
    )
```

```python
import math

import jax
import jax.numpy as jnp
import numpy as np
from jax import lax
from jax.experimental import pallas as pl
from jax.experimental.pallas import tpu as pltpu
from jax.sharding import PartitionSpec as P

QUERY_HEAD_COUNT = 64
KEY_VALUE_HEADS = 8
HEAD_SIZE = 128
BLOCK = 128
GROUP = QUERY_HEAD_COUNT // KEY_VALUE_HEADS
ROWS = GROUP * BLOCK
SLICES = 2 * KEY_VALUE_HEADS
PIECE = 8
MAX_CODE = 448.0
SCORE_SCALE = 1.0 / (HEAD_SIZE * math.sqrt(HEAD_SIZE))
BF16 = jnp.bfloat16
F32 = jnp.float32
CHUNK = 256
UNROLL = 16


def hadamard_table():
    index = np.arange(HEAD_SIZE)
    common = index[:, None] & index[None, :]
    parity = np.zeros_like(common)
    for bit in range(HEAD_SIZE.bit_length() - 1):
        parity += (common >> bit) & 1
    return np.where(parity % 2 == 0, 1.0, -1.0).astype(jnp.bfloat16)


def matmul(a, b):
    return lax.dot_general(a, b, (((1,), (0,)), ((), ())), preferred_element_type=F32)


def matmul_nt(a, b):
    return lax.dot_general(a, b, (((1,), (1,)), ((), ())), preferred_element_type=F32)


def matmul_tn(a, b):
    return lax.dot_general(a, b, (((0,), (0,)), ((), ())), preferred_element_type=F32)


def quantize(states, hadamard, inverse, factor):
    coded = jnp.clip(matmul(states, hadamard) * inverse, -MAX_CODE, MAX_CODE).astype(BF16)
    return (coded.astype(F32) * factor).astype(BF16)


def lanes(ref, head):
    return ref[:, head * HEAD_SIZE : (head + 1) * HEAD_SIZE]


def stack_heads(ref):
    return jnp.concatenate([lanes(ref, head) for head in range(GROUP)], axis=0)


def power(exponent, shift, scale):
    return jnp.left_shift(jnp.ones_like(exponent), exponent + shift).astype(F32) * scale


def own_powers(table, row):
    blocks = lax.broadcasted_iota(jnp.int32, table.shape, 1)
    level = jnp.sum(jnp.where(blocks == row, table, 0), axis=1, keepdims=True)
    return power(-level, 1, 0.5), power(level, 5, 1.0 / 32.0)


def pack_kernel(key_exponent, value_exponent, hadamard_ref, key_ref, value_ref, out_ref):
    hadamard = hadamard_ref[...]
    row = lax.axis_index("sp")

    def coded(ref, exponent_ref):
        stacked = jnp.concatenate([lanes(ref, head) for head in range(KEY_VALUE_HEADS)], axis=0)
        rotated = matmul(stacked, hadamard)
        down, up = own_powers(exponent_ref[...], row)
        parts = []
        for head in range(KEY_VALUE_HEADS):
            one = slice(head, head + 1)
            part = rotated[head * BLOCK : (head + 1) * BLOCK] * down[one, :]
            part = jnp.clip(part, -MAX_CODE, MAX_CODE).astype(BF16)
            parts.append((part.astype(F32) * up[one, :]).astype(BF16))
        return parts

    keys = coded(key_ref, key_exponent)
    values = matmul(jnp.concatenate(coded(value_ref, value_exponent), axis=0), hadamard)
    values = (values * (1.0 / HEAD_SIZE)).astype(BF16)
    for head in range(KEY_VALUE_HEADS):
        out_ref[2 * head] = keys[head]
        out_ref[2 * head + 1] = values[head * BLOCK : (head + 1) * BLOCK]


def pick_kernel(index, source_ref, out_ref):
    def some(step, carry):
        for place in range(UNROLL):
            row = step * UNROLL + place
            out_ref[row] = source_ref[index[row]]
        return carry

    lax.fori_loop(0, out_ref.shape[0] // UNROLL, some, 0)


def accumulate_kernel(index, part_ref, out_ref, even, odd):
    even[...] = jnp.zeros_like(even)
    odd[...] = jnp.zeros_like(odd)

    def some(step, carry):
        for place in range(UNROLL):
            row = step * UNROLL + place
            total = even if place % 2 == 0 else odd
            total[index[row]] += part_ref[row].astype(F32)
        return carry

    lax.fori_loop(0, part_ref.shape[0] // UNROLL, some, 0)
    out_ref[...] = (even[...] + odd[...]).astype(BF16)


def finish_kernel(own_ref, listed_ref, key_ref, value_ref):
    for head in range(KEY_VALUE_HEADS):
        cols = slice(head * HEAD_SIZE, (head + 1) * HEAD_SIZE)
        total = own_ref[2 * head : 2 * head + 2] + listed_ref[2 * head : 2 * head + 2].astype(F32)
        key_ref[:, cols] = total[0].astype(BF16)
        value_ref[:, cols] = total[1].astype(BF16)


def causal_mask():
    keys = lax.broadcasted_iota(jnp.int32, (BLOCK, ROWS), 0)
    queries = lax.broadcasted_iota(jnp.int32, (BLOCK, ROWS), 1) % BLOCK
    return keys <= queries


def own_kernel(exponent, hadamard_ref, query_ref, grad_ref, pair_ref, deq_ref, stats_ref):
    group = pl.program_id(0)
    hadamard = hadamard_ref[...]
    row = lax.axis_index("sp")
    for head in range(GROUP):
        level = exponent[row, group * GROUP + head]
        deq_ref[0, head * BLOCK : (head + 1) * BLOCK, :] = quantize(
            lanes(query_ref, head), hadamard, power(-level, 1, 0.5), power(level, 5, 1.0 / 32.0)
        )
    scores = matmul_nt(pair_ref[0], deq_ref[0]) * SCORE_SCALE
    scores = jnp.where(causal_mask(), scores, -jnp.inf)
    top = jnp.max(scores, axis=0, keepdims=True)
    weights = jnp.exp(scores - top)
    prob_grad = matmul_nt(pair_ref[1], stack_heads(grad_ref))
    stats_ref[0, 0:1, :] = top
    stats_ref[0, 1:2, :] = jnp.sum(weights, axis=0, keepdims=True)
    stats_ref[0, 2:3, :] = jnp.sum(weights * prob_grad, axis=0, keepdims=True)


def own_block():
    return lax.axis_index("blk") * lax.axis_size("sp") + lax.axis_index("sp")


def lists_other(index):
    block = own_block()
    return index[block] != block


def listed_kernel(
    index, hadamard_ref, deq_ref, grad_ref, pair_ref, stats_ref, pair_out, final_ref, score_scr, prob_scr
):
    listed = lists_other(index)

    def softmax(head, slot, start):
        cols = slice(start, start + CHUNK)
        grad = grad_rows(head, start // BLOCK, CHUNK // BLOCK)
        scores = matmul_nt(pair_ref[2 * head], deq_ref[head, cols, :])
        prob_grad = matmul_nt(pair_ref[2 * head + 1], grad)
        own_top = stats_ref[head, 0:1, cols]
        best = jnp.max(scores, axis=0, keepdims=True) * SCORE_SCALE
        top = jnp.maximum(own_top, jnp.where(listed, best, -jnp.inf))
        weights = jnp.exp(scores * SCORE_SCALE - jnp.where(listed, top, jnp.inf))
        shrink = jnp.exp(own_top - top)
        inverse = 1.0 / (
            stats_ref[head, 1:2, cols] * shrink + jnp.sum(weights, axis=0, keepdims=True)
        )
        delta = stats_ref[head, 2:3, cols] * shrink
        delta = (delta + jnp.sum(weights * prob_grad, axis=0, keepdims=True)) * inverse
        scaled = inverse * SCORE_SCALE
        prob_scr[slot, :, cols] = (weights * inverse).astype(BF16)
        score_scr[slot, :, cols] = (weights * (prob_grad * scaled - delta * scaled)).astype(BF16)
        final_ref[head, 0:1, cols] = top
        final_ref[head, 1:2, cols] = inverse
        final_ref[head, 2:3, cols] = delta

    def grad_rows(head, first, count):
        return jnp.concatenate(
            [lanes(grad_ref, head * GROUP + first + place) for place in range(count)], axis=0
        )

    for head in range(KEY_VALUE_HEADS + 1):
        if head < KEY_VALUE_HEADS:
            for start in range(0, ROWS, CHUNK):
                softmax(head, head % 2, start)
        if head > 0:
            last, slot = head - 1, (head - 1) % 2
            key_sum = matmul(score_scr[slot], deq_ref[last]).astype(BF16)
            pair_out[2 * last] = matmul(key_sum, hadamard_ref[...]).astype(BF16)
            value_sum = matmul(prob_scr[slot], grad_rows(last, 0, GROUP))
            pair_out[2 * last + 1] = value_sum.astype(BF16)


def finish_rows(array, out_ref):
    for head in range(GROUP):
        cols = slice(head * HEAD_SIZE, (head + 1) * HEAD_SIZE)
        out_ref[:, cols] = array[head * BLOCK : (head + 1) * BLOCK].astype(BF16)


def rest_kernel(
    index,
    hadamard_ref,
    deq_ref,
    grad_ref,
    own_ref,
    listed_ref,
    final_ref,
    attention_ref,
    query_grad_ref,
    pair_out,
):
    hadamard = hadamard_ref[...]
    deq = deq_ref[0]
    grad = stack_heads(grad_ref)
    top = final_ref[0, 0:1, :]
    inverse = final_ref[0, 1:2, :]
    delta = final_ref[0, 2:3, :]

    def part(key, value, mask):
        scores = matmul_nt(key, deq) * SCORE_SCALE
        probs = jnp.exp(jnp.where(mask, scores, -jnp.inf) - top) * inverse
        prob_grad = matmul_nt(value, grad)
        score_grad = (probs * (prob_grad - delta) * SCORE_SCALE).astype(BF16)
        return probs.astype(BF16), score_grad

    own_probs, own_score = part(own_ref[0], own_ref[1], causal_mask())
    listed_probs, listed_score = part(listed_ref[0], listed_ref[1], lists_other(index))
    pair_out[0] = matmul(matmul(own_score, deq).astype(BF16), hadamard)
    pair_out[1] = matmul(own_probs, grad)
    keys = jnp.concatenate([own_ref[0], listed_ref[0]], axis=0)
    keys = matmul(keys, hadamard).astype(BF16)
    values = jnp.concatenate([own_ref[1], listed_ref[1]], axis=0)
    finish_rows(matmul_tn(jnp.concatenate([own_probs, listed_probs], axis=0), values), attention_ref)
    finish_rows(matmul_tn(jnp.concatenate([own_score, listed_score], axis=0), keys), query_grad_ref)


def params(megabytes=16):
    return pltpu.CompilerParams(vmem_limit_bytes=megabytes << 20)


def smem():
    return pl.BlockSpec(memory_space=pltpu.SMEM)


def vmem():
    return pl.BlockSpec(memory_space=pltpu.VMEM)


def hbm():
    return pl.BlockSpec(memory_space=pltpu.HBM)


def shape(*dims, dtype=BF16):
    return jax.ShapeDtypeStruct(dims, dtype)


def pick(index, source):
    return pl.pallas_call(
        pick_kernel,
        out_shape=shape(*source.shape),
        in_specs=[smem(), vmem()],
        out_specs=vmem(),
        compiler_params=params(),
        name="pick",
    )(index, source)


def accumulate(index, parts):
    return pl.pallas_call(
        accumulate_kernel,
        out_shape=shape(*parts.shape),
        in_specs=[smem(), vmem()],
        out_specs=vmem(),
        scratch_shapes=[pltpu.VMEM(parts.shape, F32)] * 2,
        compiler_params=params(),
        name="accumulate",
    )(index, parts)


def pack(key_exponent, value_exponent, hadamard, keys, values):
    return pl.pallas_call(
        pack_kernel,
        out_shape=shape(SLICES, BLOCK, HEAD_SIZE),
        in_specs=[vmem()] * 5,
        out_specs=vmem(),
        compiler_params=params(60),
        name="pack",
    )(key_exponent, value_exponent, hadamard, keys, values)


def finish(own, listed):
    out = shape(BLOCK, KEY_VALUE_HEADS * HEAD_SIZE)
    return pl.pallas_call(
        finish_kernel,
        out_shape=(out, out),
        in_specs=[vmem(), vmem()],
        out_specs=(vmem(), vmem()),
        compiler_params=params(),
        name="finish",
    )(own, listed)


HADAMARD = pl.BlockSpec((HEAD_SIZE, HEAD_SIZE), lambda m: (0, 0))
TOKENS = pl.BlockSpec((BLOCK, ROWS), lambda m: (0, m))
STACKED = pl.BlockSpec((1, ROWS, HEAD_SIZE), lambda m: (m, 0, 0))
PAIR = pl.BlockSpec((2, BLOCK, HEAD_SIZE), lambda m: (m, 0, 0))
STATS = pl.BlockSpec((1, 8, ROWS), lambda m: (m, 0, 0))
STATS_SHAPE = shape(KEY_VALUE_HEADS, 8, ROWS, dtype=F32)
UNIT = 2 * BLOCK * ROWS * HEAD_SIZE * KEY_VALUE_HEADS


def cost(units, megabytes):
    return pl.CostEstimate(
        flops=units * UNIT, bytes_accessed=megabytes << 20, transcendentals=BLOCK * ROWS * KEY_VALUE_HEADS
    )


def own_part(exponent, hadamard, queries, cotangent, packed):
    return pl.pallas_call(
        own_kernel,
        grid=(KEY_VALUE_HEADS,),
        out_shape=(pltpu.HBM((KEY_VALUE_HEADS, ROWS, HEAD_SIZE), BF16), STATS_SHAPE),
        in_specs=[smem(), HADAMARD, TOKENS, TOKENS, PAIR],
        out_specs=(STACKED, STATS),
        compiler_params=params(),
        cost_estimate=cost(3, 7),
        name="own_part",
    )(exponent, hadamard, queries, cotangent, packed)


def listed_part(index, hadamard, deq, cotangent, listed, stats):
    return pl.pallas_call(
        listed_kernel,
        out_shape=(shape(SLICES, BLOCK, HEAD_SIZE), STATS_SHAPE),
        in_specs=[smem()] + [vmem()] * 5,
        out_specs=(vmem(), vmem()),
        scratch_shapes=[pltpu.VMEM((2, BLOCK, ROWS), BF16)] * 2,
        compiler_params=params(),
        cost_estimate=cost(4, 6),
        name="listed_part",
    )(index, hadamard, deq, cotangent, listed, stats)


def rest_part(index, hadamard, deq, cotangent, packed, listed, final):
    rows = shape(BLOCK, QUERY_HEAD_COUNT * HEAD_SIZE)
    sums = pltpu.HBM((SLICES, BLOCK, HEAD_SIZE), F32)
    return pl.pallas_call(
        rest_kernel,
        grid=(KEY_VALUE_HEADS,),
        out_shape=(rows, rows, sums),
        in_specs=[smem(), HADAMARD, STACKED, TOKENS, PAIR, PAIR, STATS],
        out_specs=(TOKENS, TOKENS, PAIR),
        compiler_params=params(),
        cost_estimate=cost(10, 11),
        name="rest_part",
    )(index, hadamard, deq, cotangent, packed, listed, final)


def exchange(array):
    pieces = array.reshape(-1, PIECE, HEAD_SIZE)
    return lax.all_to_all(pieces, ("blk", "sp"), split_axis=0, concat_axis=0, tiled=True)


def whole(pieces):
    return pieces.reshape(SLICES, BLOCK, HEAD_SIZE)


def local(
    queries,
    key_state_rows,
    value_state_rows,
    cotangent,
    block_list,
    query_exponent,
    key_block_exponent,
    value_block_exponent,
):
    hadamard = jnp.asarray(hadamard_table())
    index = block_list.reshape(-1)
    packed = pack(
        key_block_exponent.T, value_block_exponent.T, hadamard, key_state_rows, value_state_rows
    )
    pieces = exchange(packed)
    own = own_part(query_exponent, hadamard, queries, cotangent, packed)
    pieces, deq, stats = lax.optimization_barrier((pieces, *own))
    entries = whole(exchange(pick(index, pieces)))
    entry_pairs, final = listed_part(index, hadamard, deq, cotangent, entries, stats)
    parts = exchange(entry_pairs)
    held = pltpu.with_memory_space_constraint(deq, pltpu.HBM)
    rest = rest_part(index, hadamard, held, cotangent, packed, entries, final)
    parts, attention, query_grad, own_sums = lax.optimization_barrier((parts, *rest))
    sums = whole(exchange(accumulate(index, parts)))
    key_grad, value_grad = finish(own_sums, sums)
    return attention, query_grad, key_grad, value_grad


def solution(mesh):
    rows = P(("blk", "sp"), None)
    return jax.shard_map(
        local,
        mesh=mesh,
        in_specs=(rows, rows, rows, rows, P(), P("blk", None), P("blk", None), P("blk", None)),
        out_specs=(rows, rows, rows, rows),
        check_vma=False,
    )
```

```python
import math

import jax
import jax.numpy as jnp
import numpy as np
from jax import lax
from jax.experimental import pallas as pl
from jax.experimental.pallas import tpu as pltpu
from jax.sharding import PartitionSpec as P

QUERY_HEAD_COUNT = 64
KEY_VALUE_HEADS = 8
HEAD_SIZE = 128
BLOCK = 128
GROUP = QUERY_HEAD_COUNT // KEY_VALUE_HEADS
ROWS = GROUP * BLOCK
SLICES = 2 * KEY_VALUE_HEADS
PIECE = 8
MAX_CODE = 448.0
SCORE_SCALE = 1.0 / (HEAD_SIZE * math.sqrt(HEAD_SIZE))
LOG_SCALE = SCORE_SCALE * math.log2(math.e)
BF16 = jnp.bfloat16
F32 = jnp.float32
CHUNK = 256
UNROLL = 16


def hadamard_table():
    index = np.arange(HEAD_SIZE)
    common = index[:, None] & index[None, :]
    parity = np.zeros_like(common)
    for bit in range(HEAD_SIZE.bit_length() - 1):
        parity += (common >> bit) & 1
    return np.where(parity % 2 == 0, 1.0, -1.0).astype(jnp.bfloat16)


def matmul(a, b):
    return lax.dot_general(a, b, (((1,), (0,)), ((), ())), preferred_element_type=F32)


def matmul_nt(a, b):
    return lax.dot_general(a, b, (((1,), (1,)), ((), ())), preferred_element_type=F32)


def matmul_tn(a, b):
    return lax.dot_general(a, b, (((0,), (0,)), ((), ())), preferred_element_type=F32)


def quantize(states, hadamard, inverse, factor):
    coded = jnp.clip(matmul(states, hadamard) * inverse, -MAX_CODE, MAX_CODE).astype(BF16)
    return (coded.astype(F32) * factor).astype(BF16)


def lanes(ref, head):
    return ref[:, head * HEAD_SIZE : (head + 1) * HEAD_SIZE]


def stack_heads(ref):
    return jnp.concatenate([lanes(ref, head) for head in range(GROUP)], axis=0)


def power(exponent, shift, scale):
    return jnp.left_shift(jnp.ones_like(exponent), exponent + shift).astype(F32) * scale


def own_powers(table, row):
    blocks = lax.broadcasted_iota(jnp.int32, table.shape, 1)
    level = jnp.sum(jnp.where(blocks == row, table, 0), axis=1, keepdims=True)
    return power(-level, 1, 0.5), power(level, 5, 1.0 / 32.0)


def pack_kernel(key_exponent, value_exponent, hadamard_ref, key_ref, value_ref, out_ref):
    hadamard = hadamard_ref[...]
    row = lax.axis_index("sp")

    def coded(ref, exponent_ref):
        stacked = jnp.concatenate([lanes(ref, head) for head in range(KEY_VALUE_HEADS)], axis=0)
        rotated = matmul(stacked, hadamard)
        down, up = own_powers(exponent_ref[...], row)
        parts = []
        for head in range(KEY_VALUE_HEADS):
            one = slice(head, head + 1)
            part = rotated[head * BLOCK : (head + 1) * BLOCK] * down[one, :]
            part = jnp.clip(part, -MAX_CODE, MAX_CODE).astype(BF16)
            parts.append((part.astype(F32) * up[one, :]).astype(BF16))
        return parts

    keys = coded(key_ref, key_exponent)
    values = matmul(jnp.concatenate(coded(value_ref, value_exponent), axis=0), hadamard)
    values = (values * (1.0 / HEAD_SIZE)).astype(BF16)
    for head in range(KEY_VALUE_HEADS):
        out_ref[2 * head] = keys[head]
        out_ref[2 * head + 1] = values[head * BLOCK : (head + 1) * BLOCK]


def pick_kernel(index, source_ref, out_ref):
    for row in range(out_ref.shape[0]):
        out_ref[row] = source_ref[index[row]]


def accumulate_kernel(index, part_ref, out_ref, even, odd):
    even[...] = jnp.zeros_like(even)
    odd[...] = jnp.zeros_like(odd)

    def some(step, carry):
        for place in range(UNROLL):
            row = step * UNROLL + place
            total = even if place % 2 == 0 else odd
            total[index[row]] += part_ref[row].astype(F32)
        return carry

    lax.fori_loop(0, part_ref.shape[0] // UNROLL, some, 0)
    out_ref[...] = (even[...] + odd[...]).astype(BF16)


def finish_kernel(own_ref, listed_ref, key_ref, value_ref):
    for head in range(KEY_VALUE_HEADS // 2):
        cols = slice(head * HEAD_SIZE, (head + 1) * HEAD_SIZE)
        total = own_ref[2 * head : 2 * head + 2] + listed_ref[2 * head : 2 * head + 2].astype(F32)
        key_ref[:, cols] = total[0].astype(BF16)
        value_ref[:, cols] = total[1].astype(BF16)


def causal_mask():
    keys = lax.broadcasted_iota(jnp.int32, (BLOCK, ROWS), 0)
    queries = lax.broadcasted_iota(jnp.int32, (BLOCK, ROWS), 1) % BLOCK
    return keys <= queries


def own_kernel(exponent, hadamard_ref, query_ref, grad_ref, pair_ref, deq_ref, stats_ref):
    group = pl.program_id(0)
    hadamard = hadamard_ref[...]
    row = lax.axis_index("sp")
    for head in range(GROUP):
        level = exponent[row, group * GROUP + head]
        deq_ref[0, head * BLOCK : (head + 1) * BLOCK, :] = quantize(
            lanes(query_ref, head), hadamard, power(-level, 1, 0.5), power(level, 5, 1.0 / 32.0)
        )
    scores = matmul_nt(pair_ref[0], deq_ref[0]) * LOG_SCALE
    scores = jnp.where(causal_mask(), scores, -jnp.inf)
    top = jnp.max(scores, axis=0, keepdims=True)
    weights = jnp.exp2(scores - top)
    prob_grad = matmul_nt(pair_ref[1], stack_heads(grad_ref))
    stats_ref[0, 0:1, :] = top
    stats_ref[0, 1:2, :] = jnp.sum(weights, axis=0, keepdims=True)
    stats_ref[0, 2:3, :] = jnp.sum(weights * prob_grad, axis=0, keepdims=True)


def own_block():
    return lax.axis_index("blk") * lax.axis_size("sp") + lax.axis_index("sp")


def lists_other(index):
    block = own_block()
    return index[block] != block


def listed_kernel(
    index, hadamard_ref, deq_ref, grad_ref, pair_ref, stats_ref, pair_out, final_ref, score_scr, prob_scr
):
    listed = lists_other(index)

    def softmax(head, slot, start):
        cols = slice(start, start + CHUNK)
        grad = grad_rows(head, start // BLOCK, CHUNK // BLOCK)
        scores = matmul_nt(pair_ref[2 * head], deq_ref[head, cols, :])
        prob_grad = matmul_nt(pair_ref[2 * head + 1], grad)
        own_top = stats_ref[head, 0:1, cols]
        best = jnp.max(scores, axis=0, keepdims=True) * LOG_SCALE
        top = jnp.maximum(own_top, jnp.where(listed, best, -jnp.inf))
        weights = jnp.exp2(scores * LOG_SCALE - jnp.where(listed, top, jnp.inf))
        shrink = jnp.exp2(own_top - top)
        inverse = 1.0 / (
            stats_ref[head, 1:2, cols] * shrink + jnp.sum(weights, axis=0, keepdims=True)
        )
        delta = stats_ref[head, 2:3, cols] * shrink
        delta = (delta + jnp.sum(weights * prob_grad, axis=0, keepdims=True)) * inverse
        probs = weights * inverse
        prob_scr[slot, :, cols] = probs.astype(BF16)
        score_scr[slot, :, cols] = (probs * (prob_grad - delta)).astype(BF16)
        final_ref[head, 0:1, cols] = top
        final_ref[head, 1:2, cols] = inverse
        final_ref[head, 2:3, cols] = delta

    def grad_rows(head, first, count):
        return jnp.concatenate(
            [lanes(grad_ref, head * GROUP + first + place) for place in range(count)], axis=0
        )

    for head in range(KEY_VALUE_HEADS + 1):
        if head < KEY_VALUE_HEADS:
            for start in range(0, ROWS, CHUNK):
                softmax(head, head % 2, start)
        if head > 0:
            last, slot = head - 1, (head - 1) % 2
            key_sum = matmul(score_scr[slot], deq_ref[last]) * SCORE_SCALE
            pair_out[2 * last] = matmul(key_sum.astype(BF16), hadamard_ref[...]).astype(BF16)
            value_sum = matmul(prob_scr[slot], grad_rows(last, 0, GROUP))
            pair_out[2 * last + 1] = value_sum.astype(BF16)


def finish_rows(array, out_ref):
    for head in range(GROUP):
        cols = slice(head * HEAD_SIZE, (head + 1) * HEAD_SIZE)
        out_ref[:, cols] = array[head * BLOCK : (head + 1) * BLOCK].astype(BF16)


def rest_kernel(
    index,
    hadamard_ref,
    deq_ref,
    grad_ref,
    own_ref,
    listed_ref,
    final_ref,
    attention_ref,
    query_grad_ref,
    pair_out,
):
    hadamard = hadamard_ref[...]
    deq = deq_ref[0]
    grad = stack_heads(grad_ref)
    top = final_ref[0, 0:1, :]
    inverse = final_ref[0, 1:2, :]
    delta = final_ref[0, 2:3, :]

    def part(key, value, mask):
        scores = matmul_nt(key, deq) * LOG_SCALE
        probs = jnp.exp2(jnp.where(mask, scores, -jnp.inf) - top) * inverse
        prob_grad = matmul_nt(value, grad)
        score_grad = (probs * (prob_grad - delta) * SCORE_SCALE).astype(BF16)
        return probs.astype(BF16), score_grad

    own_probs, own_score = part(own_ref[0], own_ref[1], causal_mask())
    listed_probs, listed_score = part(listed_ref[0], listed_ref[1], lists_other(index))
    pair_out[0] = matmul(matmul(own_score, deq).astype(BF16), hadamard)
    pair_out[1] = matmul(own_probs, grad)
    keys = jnp.concatenate([own_ref[0], listed_ref[0]], axis=0)
    keys = matmul(keys, hadamard).astype(BF16)
    values = jnp.concatenate([own_ref[1], listed_ref[1]], axis=0)
    finish_rows(matmul_tn(jnp.concatenate([own_probs, listed_probs], axis=0), values), attention_ref)
    finish_rows(matmul_tn(jnp.concatenate([own_score, listed_score], axis=0), keys), query_grad_ref)


def params(megabytes=16):
    return pltpu.CompilerParams(vmem_limit_bytes=megabytes << 20)


def smem():
    return pl.BlockSpec(memory_space=pltpu.SMEM)


def vmem():
    return pl.BlockSpec(memory_space=pltpu.VMEM)


def hbm():
    return pl.BlockSpec(memory_space=pltpu.HBM)


def shape(*dims, dtype=BF16):
    return jax.ShapeDtypeStruct(dims, dtype)


def pick(index, source):
    return pl.pallas_call(
        pick_kernel,
        out_shape=shape(*source.shape),
        in_specs=[smem(), vmem()],
        out_specs=vmem(),
        compiler_params=params(),
        name="pick",
    )(index, source)


def accumulate(index, parts):
    return pl.pallas_call(
        accumulate_kernel,
        out_shape=shape(*parts.shape),
        in_specs=[smem(), vmem()],
        out_specs=vmem(),
        scratch_shapes=[pltpu.VMEM(parts.shape, F32)] * 2,
        compiler_params=params(),
        name="accumulate",
    )(index, parts)


def pack(key_exponent, value_exponent, hadamard, keys, values):
    return pl.pallas_call(
        pack_kernel,
        out_shape=shape(SLICES, BLOCK, HEAD_SIZE),
        in_specs=[vmem()] * 5,
        out_specs=vmem(),
        compiler_params=params(60),
        name="pack",
    )(key_exponent, value_exponent, hadamard, keys, values)


def finish(own, listed):
    out = shape(BLOCK, KEY_VALUE_HEADS * HEAD_SIZE)
    pairs = pl.BlockSpec((SLICES // 2, BLOCK, HEAD_SIZE), lambda half: (half, 0, 0))
    rows = pl.BlockSpec((BLOCK, KEY_VALUE_HEADS * HEAD_SIZE // 2), lambda half: (0, half))
    return pl.pallas_call(
        finish_kernel,
        grid=(2,),
        out_shape=(out, out),
        in_specs=[pairs, pairs],
        out_specs=(rows, rows),
        compiler_params=params(),
        name="finish",
    )(own, listed)


HADAMARD = pl.BlockSpec((HEAD_SIZE, HEAD_SIZE), lambda m: (0, 0))
TOKENS = pl.BlockSpec((BLOCK, ROWS), lambda m: (0, m))
STACKED = pl.BlockSpec((1, ROWS, HEAD_SIZE), lambda m: (m, 0, 0))
PAIR = pl.BlockSpec((2, BLOCK, HEAD_SIZE), lambda m: (m, 0, 0))
STATS = pl.BlockSpec((1, 8, ROWS), lambda m: (m, 0, 0))
STATS_SHAPE = shape(KEY_VALUE_HEADS, 8, ROWS, dtype=F32)
UNIT = 2 * BLOCK * ROWS * HEAD_SIZE * KEY_VALUE_HEADS


def cost(units, megabytes):
    return pl.CostEstimate(
        flops=units * UNIT, bytes_accessed=megabytes << 20, transcendentals=BLOCK * ROWS * KEY_VALUE_HEADS
    )


def own_part(exponent, hadamard, queries, cotangent, packed):
    return pl.pallas_call(
        own_kernel,
        grid=(KEY_VALUE_HEADS,),
        out_shape=(pltpu.HBM((KEY_VALUE_HEADS, ROWS, HEAD_SIZE), BF16), STATS_SHAPE),
        in_specs=[smem(), HADAMARD, TOKENS, TOKENS, PAIR],
        out_specs=(STACKED, STATS),
        compiler_params=params(),
        cost_estimate=cost(3, 7),
        name="own_part",
    )(exponent, hadamard, queries, cotangent, packed)


def listed_part(index, hadamard, deq, cotangent, listed, stats):
    return pl.pallas_call(
        listed_kernel,
        out_shape=(shape(SLICES, BLOCK, HEAD_SIZE), STATS_SHAPE),
        in_specs=[smem()] + [vmem()] * 5,
        out_specs=(vmem(), vmem()),
        scratch_shapes=[pltpu.VMEM((2, BLOCK, ROWS), BF16)] * 2,
        compiler_params=params(),
        cost_estimate=cost(4, 6),
        name="listed_part",
    )(index, hadamard, deq, cotangent, listed, stats)


def rest_part(index, hadamard, deq, cotangent, packed, listed, final):
    rows = shape(BLOCK, QUERY_HEAD_COUNT * HEAD_SIZE)
    sums = pltpu.HBM((SLICES, BLOCK, HEAD_SIZE), F32)
    return pl.pallas_call(
        rest_kernel,
        grid=(KEY_VALUE_HEADS,),
        out_shape=(rows, rows, sums),
        in_specs=[smem(), HADAMARD, STACKED, TOKENS, PAIR, PAIR, STATS],
        out_specs=(TOKENS, TOKENS, PAIR),
        compiler_params=params(),
        cost_estimate=cost(10, 11),
        name="rest_part",
    )(index, hadamard, deq, cotangent, packed, listed, final)


def exchange(array):
    pieces = array.reshape(-1, PIECE, HEAD_SIZE)
    return lax.all_to_all(pieces, ("blk", "sp"), split_axis=0, concat_axis=0, tiled=True)


def whole(pieces):
    return pieces.reshape(SLICES, BLOCK, HEAD_SIZE)


def local(
    queries,
    key_state_rows,
    value_state_rows,
    cotangent,
    block_list,
    query_exponent,
    key_block_exponent,
    value_block_exponent,
):
    hadamard = jnp.asarray(hadamard_table())
    index = block_list.reshape(-1)
    packed = pack(
        key_block_exponent.T, value_block_exponent.T, hadamard, key_state_rows, value_state_rows
    )
    pieces = exchange(packed)
    own = own_part(query_exponent, hadamard, queries, cotangent, packed)
    pieces, deq, stats = lax.optimization_barrier((pieces, *own))
    entries = whole(exchange(pick(index, pieces)))
    entry_pairs, final = listed_part(index, hadamard, deq, cotangent, entries, stats)
    parts = exchange(entry_pairs)
    held = pltpu.with_memory_space_constraint(deq, pltpu.HBM)
    rest = rest_part(index, hadamard, held, cotangent, packed, entries, final)
    parts, attention, query_grad, own_sums = lax.optimization_barrier((parts, *rest))
    sums = whole(exchange(accumulate(index, parts)))
    key_grad, value_grad = finish(own_sums, sums)
    return attention, query_grad, key_grad, value_grad


def solution(mesh):
    rows = P(("blk", "sp"), None)
    return jax.shard_map(
        local,
        mesh=mesh,
        in_specs=(rows, rows, rows, rows, P(), P("blk", None), P("blk", None), P("blk", None)),
        out_specs=(rows, rows, rows, rows),
        check_vma=False,
    )
```

```python
import math

import jax
import jax.numpy as jnp
import numpy as np
from jax import lax
from jax.experimental import pallas as pl
from jax.experimental.pallas import tpu as pltpu
from jax.sharding import PartitionSpec as P

QUERY_HEAD_COUNT = 64
KEY_VALUE_HEADS = 8
HEAD_SIZE = 128
BLOCK = 128
GROUP = QUERY_HEAD_COUNT // KEY_VALUE_HEADS
ROWS = GROUP * BLOCK
SLICES = 2 * KEY_VALUE_HEADS
PIECE = 8
MAX_CODE = 448.0
SCORE_SCALE = 1.0 / (HEAD_SIZE * math.sqrt(HEAD_SIZE))
LOG_SCALE = SCORE_SCALE * math.log2(math.e)
BF16 = jnp.bfloat16
F32 = jnp.float32
CHUNK = 256
UNROLL = 16


def hadamard_table():
    index = np.arange(HEAD_SIZE)
    common = index[:, None] & index[None, :]
    parity = np.zeros_like(common)
    for bit in range(HEAD_SIZE.bit_length() - 1):
        parity += (common >> bit) & 1
    return np.where(parity % 2 == 0, 1.0, -1.0).astype(jnp.bfloat16)


def matmul(a, b):
    return lax.dot_general(a, b, (((1,), (0,)), ((), ())), preferred_element_type=F32)


def matmul_nt(a, b):
    return lax.dot_general(a, b, (((1,), (1,)), ((), ())), preferred_element_type=F32)


def matmul_tn(a, b):
    return lax.dot_general(a, b, (((0,), (0,)), ((), ())), preferred_element_type=F32)


def quantize(states, hadamard, inverse, factor):
    coded = jnp.clip(matmul(states, hadamard) * inverse, -MAX_CODE, MAX_CODE).astype(BF16)
    return (coded.astype(F32) * factor).astype(BF16)


def lanes(ref, head):
    return ref[:, head * HEAD_SIZE : (head + 1) * HEAD_SIZE]


def stack_heads(ref):
    return jnp.concatenate([lanes(ref, head) for head in range(GROUP)], axis=0)


def power(exponent, shift, scale):
    return jnp.left_shift(jnp.ones_like(exponent), exponent + shift).astype(F32) * scale


def own_powers(table, row):
    blocks = lax.broadcasted_iota(jnp.int32, table.shape, 1)
    level = jnp.sum(jnp.where(blocks == row, table, 0), axis=1, keepdims=True)
    return power(-level, 1, 0.5), power(level, 5, 1.0 / 32.0)


def pack_kernel(key_exponent, value_exponent, hadamard_ref, key_ref, value_ref, out_ref):
    hadamard = hadamard_ref[...]
    row = lax.axis_index("sp")

    stacked = [lanes(ref, head) for ref in (value_ref, key_ref) for head in range(KEY_VALUE_HEADS)]
    rotated = matmul(jnp.concatenate(stacked, axis=0), hadamard)

    def coded(first, exponent_ref):
        down, up = own_powers(exponent_ref[...], row)
        parts = []
        for head in range(KEY_VALUE_HEADS):
            one = slice(head, head + 1)
            part = rotated[(first + head) * BLOCK : (first + head + 1) * BLOCK] * down[one, :]
            part = jnp.clip(part, -MAX_CODE, MAX_CODE).astype(BF16)
            parts.append((part.astype(F32) * up[one, :]).astype(BF16))
        return parts

    values = matmul(jnp.concatenate(coded(0, value_exponent), axis=0), hadamard)
    values = (values * (1.0 / HEAD_SIZE)).astype(BF16)
    keys = coded(KEY_VALUE_HEADS, key_exponent)
    for head in range(KEY_VALUE_HEADS):
        out_ref[2 * head] = keys[head]
        out_ref[2 * head + 1] = values[head * BLOCK : (head + 1) * BLOCK]


def pick_kernel(index, source_ref, out_ref):
    for row in range(out_ref.shape[0]):
        out_ref[row] = source_ref[index[row]]


def accumulate_kernel(index, part_ref, out_ref, even, odd):
    even[...] = jnp.zeros_like(even)
    odd[...] = jnp.zeros_like(odd)

    def some(step, carry):
        for place in range(UNROLL):
            row = step * UNROLL + place
            total = even if place % 2 == 0 else odd
            total[index[row]] += part_ref[row].astype(F32)
        return carry

    lax.fori_loop(0, part_ref.shape[0] // UNROLL, some, 0)
    out_ref[...] = (even[...] + odd[...]).astype(BF16)


def finish_kernel(own_ref, listed_ref, key_ref, value_ref):
    for head in range(KEY_VALUE_HEADS // 2):
        cols = slice(head * HEAD_SIZE, (head + 1) * HEAD_SIZE)
        total = own_ref[2 * head : 2 * head + 2] + listed_ref[2 * head : 2 * head + 2].astype(F32)
        key_ref[:, cols] = total[0].astype(BF16)
        value_ref[:, cols] = total[1].astype(BF16)


def causal_mask():
    keys = lax.broadcasted_iota(jnp.int32, (BLOCK, ROWS), 0)
    queries = lax.broadcasted_iota(jnp.int32, (BLOCK, ROWS), 1) % BLOCK
    return keys <= queries


def own_kernel(exponent, hadamard_ref, query_ref, grad_ref, pair_ref, deq_ref, stats_ref):
    group = pl.program_id(0)
    hadamard = hadamard_ref[...]
    row = lax.axis_index("sp")
    for head in range(GROUP):
        level = exponent[row, group * GROUP + head]
        deq_ref[0, head * BLOCK : (head + 1) * BLOCK, :] = quantize(
            lanes(query_ref, head), hadamard, power(-level, 1, 0.5), power(level, 5, 1.0 / 32.0)
        )
    scores = matmul_nt(pair_ref[0], deq_ref[0]) * LOG_SCALE
    scores = jnp.where(causal_mask(), scores, -jnp.inf)
    top = jnp.max(scores, axis=0, keepdims=True)
    weights = jnp.exp2(scores - top)
    prob_grad = matmul_nt(pair_ref[1], stack_heads(grad_ref))
    stats_ref[0, 0:1, :] = top
    stats_ref[0, 1:2, :] = jnp.sum(weights, axis=0, keepdims=True)
    stats_ref[0, 2:3, :] = jnp.sum(weights * prob_grad, axis=0, keepdims=True)


def own_block():
    return lax.axis_index("blk") * lax.axis_size("sp") + lax.axis_index("sp")


def lists_other(index):
    block = own_block()
    return index[block] != block


def listed_kernel(
    index, hadamard_ref, deq_ref, grad_ref, pair_ref, stats_ref, pair_out, final_ref, score_scr, prob_scr
):
    listed = lists_other(index)

    def softmax(head, slot, start):
        cols = slice(start, start + CHUNK)
        grad = grad_rows(head, start // BLOCK, CHUNK // BLOCK)
        scores = matmul_nt(pair_ref[2 * head], deq_ref[head, cols, :])
        prob_grad = matmul_nt(pair_ref[2 * head + 1], grad)
        own_top = stats_ref[head, 0:1, cols]
        best = jnp.max(scores, axis=0, keepdims=True) * LOG_SCALE
        top = jnp.maximum(own_top, jnp.where(listed, best, -jnp.inf))
        weights = jnp.exp2(scores * LOG_SCALE - jnp.where(listed, top, jnp.inf))
        shrink = jnp.exp2(own_top - top)
        inverse = 1.0 / (
            stats_ref[head, 1:2, cols] * shrink + jnp.sum(weights, axis=0, keepdims=True)
        )
        delta = stats_ref[head, 2:3, cols] * shrink
        delta = (delta + jnp.sum(weights * prob_grad, axis=0, keepdims=True)) * inverse
        probs = weights * inverse
        prob_scr[slot, :, cols] = probs.astype(BF16)
        score_scr[slot, :, cols] = (probs * (prob_grad - delta)).astype(BF16)
        final_ref[head, 0:1, cols] = top
        final_ref[head, 1:2, cols] = inverse
        final_ref[head, 2:3, cols] = delta

    def grad_rows(head, first, count):
        return jnp.concatenate(
            [lanes(grad_ref, head * GROUP + first + place) for place in range(count)], axis=0
        )

    for head in range(KEY_VALUE_HEADS + 1):
        if head < KEY_VALUE_HEADS:
            for start in range(0, ROWS, CHUNK):
                softmax(head, head % 2, start)
        if head > 0:
            last, slot = head - 1, (head - 1) % 2
            key_sum = matmul(score_scr[slot], deq_ref[last]) * SCORE_SCALE
            pair_out[2 * last] = matmul(key_sum.astype(BF16), hadamard_ref[...]).astype(BF16)
            value_sum = matmul(prob_scr[slot], grad_rows(last, 0, GROUP))
            pair_out[2 * last + 1] = value_sum.astype(BF16)


def finish_rows(array, out_ref):
    for head in range(GROUP):
        cols = slice(head * HEAD_SIZE, (head + 1) * HEAD_SIZE)
        out_ref[:, cols] = array[head * BLOCK : (head + 1) * BLOCK].astype(BF16)


def rest_kernel(
    index,
    hadamard_ref,
    deq_ref,
    grad_ref,
    own_ref,
    listed_ref,
    final_ref,
    attention_ref,
    query_grad_ref,
    pair_out,
):
    hadamard = hadamard_ref[...]
    deq = deq_ref[0]
    grad = stack_heads(grad_ref)
    top = final_ref[0, 0:1, :]
    inverse = final_ref[0, 1:2, :]
    delta = final_ref[0, 2:3, :]

    def part(key, value, mask):
        scores = matmul_nt(key, deq) * LOG_SCALE
        probs = jnp.exp2(jnp.where(mask, scores, -jnp.inf) - top) * inverse
        prob_grad = matmul_nt(value, grad)
        score_grad = (probs * (prob_grad - delta) * SCORE_SCALE).astype(BF16)
        return probs.astype(BF16), score_grad

    own_probs, own_score = part(own_ref[0], own_ref[1], causal_mask())
    listed_probs, listed_score = part(listed_ref[0], listed_ref[1], lists_other(index))
    pair_out[0] = matmul(matmul(own_score, deq).astype(BF16), hadamard)
    pair_out[1] = matmul(own_probs, grad)
    keys = jnp.concatenate([own_ref[0], listed_ref[0]], axis=0)
    keys = matmul(keys, hadamard).astype(BF16)
    values = jnp.concatenate([own_ref[1], listed_ref[1]], axis=0)
    finish_rows(matmul_tn(jnp.concatenate([own_probs, listed_probs], axis=0), values), attention_ref)
    finish_rows(matmul_tn(jnp.concatenate([own_score, listed_score], axis=0), keys), query_grad_ref)


def params(megabytes=16):
    return pltpu.CompilerParams(vmem_limit_bytes=megabytes << 20)


def smem():
    return pl.BlockSpec(memory_space=pltpu.SMEM)


def vmem():
    return pl.BlockSpec(memory_space=pltpu.VMEM)


def hbm():
    return pl.BlockSpec(memory_space=pltpu.HBM)


def shape(*dims, dtype=BF16):
    return jax.ShapeDtypeStruct(dims, dtype)


def pick(index, source):
    return pl.pallas_call(
        pick_kernel,
        out_shape=shape(*source.shape),
        in_specs=[smem(), vmem()],
        out_specs=vmem(),
        compiler_params=params(),
        name="pick",
    )(index, source)


def accumulate(index, parts):
    return pl.pallas_call(
        accumulate_kernel,
        out_shape=shape(*parts.shape),
        in_specs=[smem(), vmem()],
        out_specs=vmem(),
        scratch_shapes=[pltpu.VMEM(parts.shape, F32)] * 2,
        compiler_params=params(),
        name="accumulate",
    )(index, parts)


def pack(key_exponent, value_exponent, hadamard, keys, values):
    return pl.pallas_call(
        pack_kernel,
        out_shape=shape(SLICES, BLOCK, HEAD_SIZE),
        in_specs=[vmem()] * 5,
        out_specs=vmem(),
        compiler_params=params(60),
        name="pack",
    )(key_exponent, value_exponent, hadamard, keys, values)


def finish(own, listed):
    out = shape(BLOCK, KEY_VALUE_HEADS * HEAD_SIZE)
    pairs = pl.BlockSpec((SLICES // 2, BLOCK, HEAD_SIZE), lambda half: (half, 0, 0))
    rows = pl.BlockSpec((BLOCK, KEY_VALUE_HEADS * HEAD_SIZE // 2), lambda half: (0, half))
    return pl.pallas_call(
        finish_kernel,
        grid=(2,),
        out_shape=(out, out),
        in_specs=[pairs, pairs],
        out_specs=(rows, rows),
        compiler_params=params(),
        name="finish",
    )(own, listed)


HADAMARD = pl.BlockSpec((HEAD_SIZE, HEAD_SIZE), lambda m: (0, 0))
TOKENS = pl.BlockSpec((BLOCK, ROWS), lambda m: (0, m))
STACKED = pl.BlockSpec((1, ROWS, HEAD_SIZE), lambda m: (m, 0, 0))
PAIR = pl.BlockSpec((2, BLOCK, HEAD_SIZE), lambda m: (m, 0, 0))
STATS = pl.BlockSpec((1, 8, ROWS), lambda m: (m, 0, 0))
STATS_SHAPE = shape(KEY_VALUE_HEADS, 8, ROWS, dtype=F32)
UNIT = 2 * BLOCK * ROWS * HEAD_SIZE * KEY_VALUE_HEADS


def cost(units, megabytes):
    return pl.CostEstimate(
        flops=units * UNIT, bytes_accessed=megabytes << 20, transcendentals=BLOCK * ROWS * KEY_VALUE_HEADS
    )


def own_part(exponent, hadamard, queries, cotangent, packed):
    return pl.pallas_call(
        own_kernel,
        grid=(KEY_VALUE_HEADS,),
        out_shape=(pltpu.HBM((KEY_VALUE_HEADS, ROWS, HEAD_SIZE), BF16), STATS_SHAPE),
        in_specs=[smem(), HADAMARD, TOKENS, TOKENS, PAIR],
        out_specs=(STACKED, STATS),
        compiler_params=params(),
        cost_estimate=cost(3, 7),
        name="own_part",
    )(exponent, hadamard, queries, cotangent, packed)


def listed_part(index, hadamard, deq, cotangent, listed, stats):
    return pl.pallas_call(
        listed_kernel,
        out_shape=(shape(SLICES, BLOCK, HEAD_SIZE), STATS_SHAPE),
        in_specs=[smem()] + [vmem()] * 5,
        out_specs=(vmem(), vmem()),
        scratch_shapes=[pltpu.VMEM((2, BLOCK, ROWS), BF16)] * 2,
        compiler_params=params(),
        cost_estimate=cost(4, 6),
        name="listed_part",
    )(index, hadamard, deq, cotangent, listed, stats)


def rest_part(index, hadamard, deq, cotangent, packed, listed, final):
    rows = shape(BLOCK, QUERY_HEAD_COUNT * HEAD_SIZE)
    sums = pltpu.HBM((SLICES, BLOCK, HEAD_SIZE), F32)
    return pl.pallas_call(
        rest_kernel,
        grid=(KEY_VALUE_HEADS,),
        out_shape=(rows, rows, sums),
        in_specs=[smem(), HADAMARD, STACKED, TOKENS, PAIR, PAIR, STATS],
        out_specs=(TOKENS, TOKENS, PAIR),
        compiler_params=params(),
        cost_estimate=cost(10, 11),
        name="rest_part",
    )(index, hadamard, deq, cotangent, packed, listed, final)


def exchange(array):
    pieces = array.reshape(-1, PIECE, HEAD_SIZE)
    return lax.all_to_all(pieces, ("blk", "sp"), split_axis=0, concat_axis=0, tiled=True)


def whole(pieces):
    return pieces.reshape(SLICES, BLOCK, HEAD_SIZE)


def local(
    queries,
    key_state_rows,
    value_state_rows,
    cotangent,
    block_list,
    query_exponent,
    key_block_exponent,
    value_block_exponent,
):
    hadamard = jnp.asarray(hadamard_table())
    index = block_list.reshape(-1)
    packed = pack(
        key_block_exponent.T, value_block_exponent.T, hadamard, key_state_rows, value_state_rows
    )
    pieces = exchange(packed)
    own = own_part(query_exponent, hadamard, queries, cotangent, packed)
    pieces, deq, stats = lax.optimization_barrier((pieces, *own))
    entries = whole(exchange(pick(index, pieces)))
    entry_pairs, final = listed_part(index, hadamard, deq, cotangent, entries, stats)
    parts = exchange(entry_pairs)
    held = pltpu.with_memory_space_constraint(deq, pltpu.HBM)
    rest = rest_part(index, hadamard, held, cotangent, packed, entries, final)
    parts, attention, query_grad, own_sums = lax.optimization_barrier((parts, *rest))
    sums = whole(exchange(accumulate(index, parts)))
    key_grad, value_grad = finish(own_sums, sums)
    return attention, query_grad, key_grad, value_grad


def solution(mesh):
    rows = P(("blk", "sp"), None)
    return jax.shard_map(
        local,
        mesh=mesh,
        in_specs=(rows, rows, rows, rows, P(), P("blk", None), P("blk", None), P("blk", None)),
        out_specs=(rows, rows, rows, rows),
        check_vma=False,
    )
```
